512 devices in a mesh: ctx: 64 (over y, x, core), pp: 8 (over z).
Axes of the slice: x: 4, y: 8, z: 8, core: 2. Of those that a mesh axis runs over, the one named last changes fastest.
Arguments:
- inputs: bfloat16 [8, 2, 4096, 2048], P('pp', None, 'ctx'), may hold values from -6 to 6
- saved_keys: bfloat16 [8, 2, 4096, 512], P('pp', None, 'ctx'), may hold values from -6 to 6
- saved_values: bfloat16 [8, 2, 4096, 512], P('pp', None, 'ctx'), may hold values from -5 to 5
- query_gain: float32 [8, 2048], P('pp'), may hold values from 0.25 to 1.75
- first_grads: bfloat16 [8, 4096, 2048], P('pp', 'ctx'), may hold values from -5 to 5
- head_grads: bfloat16 [1, 4096, 2048], P(None, 'ctx'), may hold values from -5 to 5
- window: int32 [8, 4], P('pp'), may hold values from 1 to 7, as said below
- stride: int32 [8, 4], P('pp'), may hold values from 16 to 32, as said below
Outputs:
- grads_out: bfloat16 [8, 2, 4096, 2048], P('pp', None, 'ctx')
- key_grads: bfloat16 [8, 2, 4096, 512], P('pp', None, 'ctx')
- value_grads: bfloat16 [8, 2, 4096, 512], P('pp', None, 'ctx')
The draws below stay inside these ranges and needn't reach their ends.
Inputs may be any that keep to these rules, and one draw needn't show every extreme that they name: `window`: every entry is 1 to 7; some entry equals 7 and some equals 1. `stride`: every entry is 16 or 32; both occur.
All inputs are finite; a program needn't handle non-finite values.
Results may differ from the reference program's by a relative error of at most 0.014.
Values may be sent and summed in bfloat16 or wider, within the bound.
No kernel may reach another device: no remote copies, remote signals or barrier semaphores. Data moves between devices by JAX's collectives and lax.ppermute only.
A program may use at most 64 MiB of HBM per device.

```python
import jax
import jax.numpy as jnp
from jax import lax

BLK = 64
WIN = 7
STRIDE = 16
TICKS = 2
KV_HEADS = 4
HEAD_DIM = 128
GROUP = 4
FEAT = 2048
KVW = 512
SEQ = 4096
SUMMARY = 4
LAYERS = 8
N_CTX = 64


def draw_inputs(key, part):
    key = jax.random.fold_in(key, 11)
    base = jnp.clip(jax.random.normal(key, (LAYERS, TICKS, SEQ, FEAT), jnp.float32), -4.0, 4.0)
    return base.astype(jnp.bfloat16)


def draw_saved_keys(key, part):
    key = jax.random.fold_in(key, 12)
    base = jnp.clip(jax.random.normal(key, (LAYERS, TICKS, SEQ, KVW), jnp.float32), -4.0, 4.0)
    return base.astype(jnp.bfloat16)


def draw_window(key, part):
    key = jax.random.fold_in(key, 13)
    values = jax.random.randint(key, (LAYERS * KV_HEADS,), 1, WIN + 1)
    order = jax.random.permutation(jax.random.fold_in(key, 1), LAYERS * KV_HEADS)
    values = values.at[order[0]].set(WIN).at[order[1]].set(1)
    return values.reshape(LAYERS, KV_HEADS).astype(jnp.int32)


def draw_stride(key, part):
    key = jax.random.fold_in(key, 14)
    values = STRIDE * (1 + jax.random.randint(key, (LAYERS * KV_HEADS,), 0, 2))
    order = jax.random.permutation(jax.random.fold_in(key, 1), LAYERS * KV_HEADS)
    values = values.at[order[0]].set(STRIDE).at[order[1]].set(2 * STRIDE)
    return values.reshape(LAYERS, KV_HEADS).astype(jnp.int32)


def block_levels(rng, shape, split, low, top_value):
    level = 1.0
    for axis_at, shards_of in split:
        heights = jax.random.uniform(jax.random.fold_in(jax.random.fold_in(rng, 6), axis_at), (shards_of,), jnp.float32, low / len(split), top_value / len(split))
        level = level * jnp.repeat(jnp.exp(heights), shape[axis_at] // shards_of).reshape((-1,) + (1,) * (len(shape) - 1 - axis_at))
    return level


def normal_values(rng, shape, deviation, reach, shards=(), held_as=jnp.bfloat16):
    loudness = block_levels(rng, shape, shards, -0.22, 0.18) if shards else 1.0
    values = jax.random.normal(rng, shape, jnp.float32) * deviation * loudness
    return jnp.minimum(jnp.maximum(values, -reach), reach).astype(held_as)


def setup_inputs(seed: int = 0) -> dict:
    streams_of = jax.random.split(jax.random.key(seed), 9)
    return {
        "inputs": draw_inputs(jax.random.fold_in(streams_of[8], 71), 0),
        "saved_keys": draw_saved_keys(jax.random.fold_in(streams_of[8], 71), 0),
        "saved_values": normal_values(streams_of[2], (LAYERS, TICKS, SEQ, KVW), 1.0, 5.0, ((0, 8), (2, 64))),
        "query_gain": jnp.clip(1.0 + 0.15 * jax.random.normal(streams_of[3], (LAYERS, FEAT), jnp.float32), 0.25, 1.75),
        "first_grads": normal_values(streams_of[4], (LAYERS, SEQ, FEAT), 1.0, 5.0, ((0, 8), (1, 64))),
        "head_grads": normal_values(streams_of[5], (TICKS - 1, SEQ, FEAT), 1.0, 5.0, ((1, 64),)),
        "window": draw_window(jax.random.fold_in(streams_of[8], 71), 0),
        "stride": draw_stride(jax.random.fold_in(streams_of[8], 71), 0),
    }


def block_allowed(block, window, stride, summary_count):
    row_ids = jnp.arange(BLK, dtype=jnp.int32)
    query_pos = block * BLK + row_ids
    col_ids = jnp.arange(WIN * BLK, dtype=jnp.int32)
    key_block = block - WIN + 1 + col_ids // BLK
    key_pos = (block - WIN + 1) * BLK + col_ids
    local_ok = (key_block[None, None, :] >= 0) & (key_pos[None, None, :] <= query_pos[None, :, None])
    local_ok = local_ok & ((block - key_block)[None, None, :] < window[:, None, None])
    strided_block = STRIDE * (jnp.arange(summary_count * BLK, dtype=jnp.int32) // BLK)
    strided_ok = (strided_block[None, None, :] % stride[:, None, None] == 0)
    strided_ok = strided_ok & (strided_block[None, None, :] <= block - window[:, None, None])
    heads = window.shape[0]
    local_ok = jnp.broadcast_to(local_ok, (heads, BLK, WIN * BLK))
    strided_ok = jnp.broadcast_to(strided_ok, (heads, BLK, summary_count * BLK))
    return jnp.concatenate([local_ok, strided_ok], axis=2)


def layer_backward(inputs, saved_keys, saved_values, gain, grad_out, window, stride):
    scale = HEAD_DIM ** -0.5
    queries = (inputs.astype(jnp.float32) * gain).astype(jnp.bfloat16)
    paired = jnp.concatenate([saved_keys, saved_values], axis=1)
    padded = jnp.concatenate([jnp.zeros(((WIN - 1) * BLK, 2 * KVW), jnp.bfloat16), paired], axis=0)
    summary = paired.reshape(N_CTX, BLK, 2 * KVW)[::STRIDE].reshape(SUMMARY * BLK, 2 * KVW)
    keys_total = (WIN + SUMMARY) * BLK

    def one_block(block):
        local = lax.dynamic_slice_in_dim(padded, block * BLK, WIN * BLK, 0)
        kv_all = jnp.concatenate([local, summary], axis=0).astype(jnp.float32)
        key_all = kv_all[:, :KVW].reshape(keys_total, KV_HEADS, HEAD_DIM)
        value_all = kv_all[:, KVW:].reshape(keys_total, KV_HEADS, HEAD_DIM)
        query_blk = lax.dynamic_slice_in_dim(queries, block * BLK, BLK, 0)
        query_blk = query_blk.astype(jnp.float32).reshape(BLK, KV_HEADS, GROUP, HEAD_DIM)
        grad_blk = lax.dynamic_slice_in_dim(grad_out, block * BLK, BLK, 0)
        grad_blk = grad_blk.astype(jnp.float32).reshape(BLK, KV_HEADS, GROUP, HEAD_DIM)
        allowed = block_allowed(block, window, stride, SUMMARY)[:, None]
        scores = jnp.einsum("qhgd,khd->hgqk", query_blk, key_all) * scale
        scores = jnp.where(allowed, scores, jnp.float32(-1e30))
        row_peak = jnp.max(scores, axis=3, keepdims=True)
        weights = jnp.exp(scores - row_peak)
        probs = weights / jnp.sum(weights, axis=3, keepdims=True)
        grad_prob = jnp.einsum("qhgd,khd->hgqk", grad_blk, value_all)
        row_delta = jnp.sum(probs * grad_prob, axis=3, keepdims=True)
        dscore = (probs * (grad_prob - row_delta) * scale).astype(jnp.bfloat16).astype(jnp.float32)
        probs_round = probs.astype(jnp.bfloat16).astype(jnp.float32)
        dquery = jnp.einsum("hgqk,khd->qhgd", dscore, key_all).reshape(BLK, FEAT)
        key_grad = jnp.einsum("hgqk,qhgd->khd", dscore, query_blk).reshape(keys_total, KVW)
        value_grad = jnp.einsum("hgqk,qhgd->khd", probs_round, grad_blk).reshape(keys_total, KVW)
        return dquery, jnp.concatenate([key_grad, value_grad], axis=1)

    dquery_all, parts = lax.map(one_block, jnp.arange(N_CTX, dtype=jnp.int32))
    result = (grad_out.astype(jnp.float32) + gain * dquery_all.reshape(SEQ, FEAT)).astype(jnp.bfloat16)
    local_parts = parts[:, :WIN * BLK].reshape(N_CTX, WIN, BLK, 2 * KVW)
    total = local_parts[:, WIN - 1]
    for offset in range(1, WIN):
        shifted = jnp.concatenate([local_parts[offset:, WIN - 1 - offset], jnp.zeros((offset, BLK, 2 * KVW), jnp.float32)], axis=0)
        total = total + lax.optimization_barrier(shifted.astype(jnp.bfloat16)).astype(jnp.float32)
    strided_sum = jnp.sum(parts[:, WIN * BLK:], axis=0).reshape(SUMMARY, BLK, 2 * KVW)
    total = total.reshape(SUMMARY, STRIDE, BLK, 2 * KVW).at[:, 0].add(strided_sum).reshape(SEQ, 2 * KVW)
    return result, total[:, :KVW].astype(jnp.bfloat16), total[:, KVW:].astype(jnp.bfloat16)


def reference(inputs, saved_keys, saved_values, query_gain, first_grads, head_grads, window, stride):
    grad_table = [[None] * TICKS for layer in range(LAYERS)]
    key_table = [[None] * TICKS for layer in range(LAYERS)]
    value_table = [[None] * TICKS for layer in range(LAYERS)]
    for step_index in range(TICKS):
        for layer in range(LAYERS):
            if step_index == 0:
                grad_out = first_grads[layer]
            elif layer == LAYERS - 1:
                grad_out = head_grads[step_index - 1]
            else:
                grad_out = grad_table[layer + 1][step_index - 1]
            result, key_grad, value_grad = layer_backward(inputs[layer, step_index], saved_keys[layer, step_index], saved_values[layer, step_index], query_gain[layer], grad_out, window[layer], stride[layer])
            grad_table[layer][step_index] = result
            key_table[layer][step_index] = key_grad
            value_table[layer][step_index] = value_grad
    grads_out = jnp.stack([jnp.stack(row, 0) for row in grad_table], 0)
    key_grads = jnp.stack([jnp.stack(row, 0) for row in key_table], 0)
    value_grads = jnp.stack([jnp.stack(row, 0) for row in value_table], 0)
    return grads_out, key_grads, value_grads
```

```python
import functools

import jax
import jax.numpy as jnp
from jax import lax
from jax.experimental import pallas as pl
from jax.experimental.pallas import tpu as pltpu
from jax.sharding import PartitionSpec as P

BLK = 64
WIN = 7
STRIDE = 16
HEAD_DIM = 128
GROUP = 4
HALF_HEADS = 2
HALF_KV = HALF_HEADS * HEAD_DIM
HALF_FEAT = HALF_HEADS * GROUP * HEAD_DIM
SCALE = HEAD_DIM**-0.5
LOG2E = 1.4426950408889634
NEG = -1e30
NT = (((1,), (1,)), ((), ()))
TN = (((0,), (0,)), ((), ()))


def route(array, axis, move):
    size = lax.axis_size(axis)
    pairs = [(i, move(i)) for i in range(size)]
    return lax.ppermute(array, axis, [(a, b) for a, b in pairs if b is not None and 0 <= b < size])


def sibling(array):
    return route(array, "ctx", lambda i: i ^ 1)


def attention_kernel(has_head, *refs):
    meta, gain, q_mine, q_other, g_mine, g_other = refs[:6]
    refs = refs[6:]
    if has_head:
        h_mine, h_other = refs[:2]
        refs = refs[2:]
    pairs, strided = refs[:4], refs[4:8]
    result, own, back1, back2, back3, part0, part1, part2, part3 = refs[8:]
    backs = (own, back1, back2, back3)
    parts = (part0, part1, part2, part3)
    index = meta[0]
    blocks = (index, jnp.bitwise_xor(index, 1))
    group = index // STRIDE
    for h in range(HALF_HEADS):
        window = meta[2 + h]
        stride = meta[4 + h]
        q_rows, g_rows = [], []
        for half, (q_ref, g_ref) in enumerate(((q_mine, g_mine), (q_other, g_other))):
            for j in range(GROUP):
                at = slice((h * GROUP + j) * HEAD_DIM, (h * GROUP + j + 1) * HEAD_DIM)
                q_rows.append((q_ref[:, at].astype(jnp.float32) * gain[:, at]).astype(jnp.bfloat16))
                grad = g_ref[:, at]
                if has_head:
                    top = (h_mine, h_other)[half][:, at]
                    grad = jnp.where(meta[1] == 1, top, grad)
                g_rows.append(grad)
        q = jnp.concatenate(q_rows, axis=0)
        g = jnp.concatenate(g_rows, axis=0)
        k_at = slice(h * HEAD_DIM, (h + 1) * HEAD_DIM)
        v_at = slice(HALF_KV + h * HEAD_DIM, HALF_KV + (h + 1) * HEAD_DIM)
        k = jnp.concatenate([r[:, k_at] for r in pairs + strided], axis=0)
        v = jnp.concatenate([r[:, v_at] for r in pairs + strided], axis=0)
        scores = lax.dot_general(k, q, NT, preferred_element_type=jnp.float32)
        wide = GROUP * BLK
        key_row = lax.broadcasted_iota(jnp.int32, (BLK, wide), 0)
        query_row = lax.broadcasted_iota(jnp.int32, (BLK, wide), 1) % BLK
        rows = []
        for slot in range(12):
            cells = []
            for half in range(2):
                query_block = blocks[half]
                if slot < 8:
                    key_block = blocks[slot % 2] - 2 * (slot // 2)
                    gap = query_block - key_block
                    ok = (key_block >= 0) & (gap >= 0) & (gap < WIN)
                    ok = ok & ((gap < window) | (key_block % stride == 0))
                else:
                    key_block = STRIDE * (group - (slot - 8))
                    ok = (key_block >= 0) & (key_block <= query_block - WIN)
                    ok = ok & (key_block % stride == 0)
                cell = scores[slot * BLK : (slot + 1) * BLK, half * wide : (half + 1) * wide]
                if slot == half:
                    cell = jnp.where(key_row <= query_row, cell, NEG)
                else:
                    cell = jnp.where(ok, cell, NEG)
                cells.append(cell)
            rows.append(jnp.concatenate(cells, axis=1))
        scores = jnp.concatenate(rows, axis=0)
        peak = jnp.max(scores, axis=0, keepdims=True)
        weights = jnp.exp2((scores - peak) * (SCALE * LOG2E))
        probs = weights * (1.0 / jnp.sum(weights, axis=0, keepdims=True))
        grad_prob = lax.dot_general(v, g, NT, preferred_element_type=jnp.float32)
        delta = jnp.sum(probs * grad_prob, axis=0, keepdims=True)
        dscore = (probs * (grad_prob - delta)).astype(jnp.bfloat16)
        dquery = lax.dot_general(dscore, k, TN, preferred_element_type=jnp.float32) * SCALE
        dkey = jnp.dot(dscore, q, preferred_element_type=jnp.float32) * SCALE
        dvalue = jnp.dot(probs.astype(jnp.bfloat16), g, preferred_element_type=jnp.float32)
        for half in range(2):
            for j in range(GROUP):
                at = slice((h * GROUP + j) * HEAD_DIM, (h * GROUP + j + 1) * HEAD_DIM)
                row = (half * GROUP + j) * BLK
                grad = g[row : row + BLK].astype(jnp.float32)
                total = grad + gain[:, at] * dquery[row : row + BLK]
                result[half, :, at] = total.astype(jnp.bfloat16)
        for d in range(4):
            rows_at = slice(2 * BLK * d, 2 * BLK * (d + 1))
            backs[d][:, k_at] = dkey[rows_at].astype(backs[d].dtype)
            backs[d][:, v_at] = dvalue[rows_at].astype(backs[d].dtype)
        for s in range(4):
            rows_at = slice(8 * BLK + BLK * s, 8 * BLK + BLK * (s + 1))
            parts[s][:, k_at] = dkey[rows_at].astype(parts[s].dtype)
            parts[s][:, v_at] = dvalue[rows_at].astype(parts[s].dtype)


def attention(tick, meta, gain, keep, recv, grads, pairs, strided):
    wide = 2 * HALF_KV

    def at(lead, *rest):
        return pl.BlockSpec((None,) + rest, lambda n: (lead, 0, 0))

    whole = pl.BlockSpec(memory_space=pltpu.VMEM)
    args = [meta, gain, keep, recv]
    specs = [
        pl.BlockSpec(memory_space=pltpu.SMEM),
        whole,
        at(tick, BLK, HALF_FEAT),
        at(tick, BLK, HALF_FEAT),
    ]
    if grads is None:
        args += [keep, recv]
        specs += [at(2, BLK, HALF_FEAT), at(2, BLK, HALF_FEAT)]
    else:
        args += [grads, grads, keep, recv]
        specs += [at(0, BLK, HALF_FEAT), at(1, BLK, HALF_FEAT)]
        specs += [at(3, BLK, HALF_FEAT), at(3, BLK, HALF_FEAT)]
    args += list(pairs) + list(strided)
    specs += [at(tick, 2 * BLK, wide)] * 4 + [at(tick, BLK, wide)] * 4
    bf16, f32 = jnp.bfloat16, jnp.float32
    out_shape = [
        jax.ShapeDtypeStruct((2, BLK, HALF_FEAT), bf16),
        jax.ShapeDtypeStruct((2 * BLK, wide), f32),
        jax.ShapeDtypeStruct((2 * BLK, wide), bf16),
        jax.ShapeDtypeStruct((2 * BLK, wide), bf16),
        jax.ShapeDtypeStruct((2 * BLK, wide), bf16),
        jax.ShapeDtypeStruct((BLK, wide), f32),
        jax.ShapeDtypeStruct((BLK, wide), bf16),
        jax.ShapeDtypeStruct((BLK, wide), bf16),
        jax.ShapeDtypeStruct((BLK, wide), bf16),
    ]
    return pl.pallas_call(
        functools.partial(attention_kernel, grads is not None),
        out_shape=out_shape,
        grid=(1,),
        in_specs=specs,
        out_specs=[whole] * len(out_shape),
        compiler_params=pltpu.CompilerParams(vmem_limit_bytes=32 << 20),
        cost_estimate=pl.CostEstimate(
            flops=2 * 5 * 2 * 512 * 768 * 128, bytes_accessed=4 << 20, transcendentals=2 * 512 * 768
        ),
        name="attention",
    )(*args)


def body(inputs, saved_keys, saved_values, query_gain, first_grads, head_grads, window, stride):
    index = lax.axis_index("ctx")
    section = lax.axis_index("pp")
    last = lax.axis_size("pp") - 1
    core = index % 2
    place = (index // 2) % 4
    even_row = (index // 8) % 2 == 0
    ticks = inputs.shape[1]
    f32, bf16 = jnp.float32, jnp.bfloat16

    def halves(array):
        cut = array.shape[-1] // 2
        low, high = array[..., :cut], array[..., cut:]
        return jnp.where(core == 0, low, high), jnp.where(core == 0, high, low)

    key_keep, key_give = halves(saved_keys[0])
    value_keep, value_give = halves(saved_values[0])
    kv_keep = jnp.concatenate([key_keep, value_keep], axis=-1)
    kv_recv = sibling(jnp.concatenate([key_give, value_give], axis=-1))
    stacked = jnp.concatenate([inputs[0], first_grads, head_grads], axis=0)
    keep, give = halves(stacked)
    recv = sibling(give)
    gain = jnp.where(core == 0, query_gain[:, :HALF_FEAT], query_gain[:, HALF_FEAT:])
    heads = jnp.where(core == 0, window[0, :2], window[0, 2:])
    steps = jnp.where(core == 0, stride[0, :2], stride[0, 2:])
    top = jnp.where(section == last, 1, 0)
    meta = jnp.concatenate([jnp.stack([index, top]).astype(jnp.int32), heads, steps])

    pair = jnp.concatenate([kv_keep, kv_recv], axis=1)
    pairs = [pair]
    for d in range(1, 4):
        pairs.append(route(pair, "ctx", lambda i: i + 2 * d))

    def pick(array):
        return jnp.where(core == 0, array[:, :BLK], array[:, BLK:])

    chosen = pick(pairs[0])
    for d in range(1, 4):
        chosen = jnp.where(place == d, pick(pairs[d]), chosen)
    above = route(chosen, "ctx", lambda i: i + 8 if (i // 8) % 2 == 0 else None)
    chosen = jnp.where(even_row, chosen, above)
    strided = [chosen]
    for s in range(1, 4):
        strided.append(route(chosen, "ctx", lambda i: i + STRIDE * s))

    results, totals = [], []
    grads = None
    for tick in range(ticks):
        outs = attention(tick, meta, gain, keep, recv, grads, pairs, strided)
        result, own, backs, parts = outs[0], outs[1], outs[2:5], outs[5:9]
        if tick < ticks - 1:
            grads = route(result, "pp", lambda i: i - 1)
        results.append(result)
        total = parts[0]
        for s in range(1, 4):
            total = total + route(parts[s], "ctx", lambda i: i - STRIDE * s).astype(f32)
        below = route(
            total.astype(bf16), "ctx", lambda i: i - 8 if (i // 8) % 2 == 1 else None
        )
        total = jnp.where(even_row, total + below.astype(f32), 0.0)
        zero = jnp.zeros_like(total)
        spread = jnp.concatenate(
            [jnp.where(core == 0, total, zero), jnp.where(core == 0, zero, total)], axis=0
        )
        final = own + jnp.where(place == 0, spread, 0.0)
        for d in range(1, 4):
            piece = backs[d - 1].astype(f32) + jnp.where(place == d, spread, 0.0)
            final = final + route(piece.astype(bf16), "ctx", lambda i: i - 2 * d).astype(f32)
        totals.append(final.astype(bf16))

    def join(mine, other):
        return jnp.concatenate(
            [jnp.where(core == 0, mine, other), jnp.where(core == 0, other, mine)], axis=-1
        )

    grads_out = [join(r[0], sibling(r[1])) for r in results]
    key_grads, value_grads = [], []
    for total in totals:
        mine, other = total[:BLK], sibling(total[BLK:])
        key_grads.append(join(mine[:, :HALF_KV], other[:, :HALF_KV]))
        value_grads.append(join(mine[:, HALF_KV:], other[:, HALF_KV:]))
    return (
        jnp.stack(grads_out, axis=0)[None],
        jnp.stack(key_grads, axis=0)[None],
        jnp.stack(value_grads, axis=0)[None],
    )


def solution(mesh):
    in_specs = (
        P("pp", None, "ctx", None),
        P("pp", None, "ctx", None),
        P("pp", None, "ctx", None),
        P("pp", None),
        P("pp", "ctx", None),
        P(None, "ctx", None),
        P("pp", None),
        P("pp", None),
    )
    out_specs = (P("pp", None, "ctx", None), P("pp", None, "ctx", None), P("pp", None, "ctx", None))
    return jax.shard_map(body, mesh=mesh, in_specs=in_specs, out_specs=out_specs, check_vma=False)
```

```python
import functools

import jax
import jax.numpy as jnp
from jax import lax
from jax.experimental import pallas as pl
from jax.experimental.pallas import tpu as pltpu
from jax.sharding import PartitionSpec as P

BLK = 64
WIN = 7
STRIDE = 16
HEAD_DIM = 128
GROUP = 4
HALF_HEADS = 2
HALF_KV = HALF_HEADS * HEAD_DIM
HALF_FEAT = HALF_HEADS * GROUP * HEAD_DIM
SCALE = HEAD_DIM**-0.5
LOG2E = 1.4426950408889634
NEG = -1e30
NT = (((1,), (1,)), ((), ()))
TN = (((0,), (0,)), ((), ()))


def route(array, axis, move):
    size = lax.axis_size(axis)
    pairs = [(i, move(i)) for i in range(size)]
    return lax.ppermute(array, axis, [(a, b) for a, b in pairs if b is not None and 0 <= b < size])


def sibling(array):
    return route(array, "ctx", lambda i: i ^ 1)


def attention_kernel(has_head, *refs):
    meta, gain, q_mine, q_other, g_mine, g_other = refs[:6]
    refs = refs[6:]
    if has_head:
        h_mine, h_other = refs[:2]
        refs = refs[2:]
    pairs, strided = refs[:4], refs[4:8]
    refs = refs[8:]
    if has_head:
        for old, new in zip(refs[:4], refs[5:9]):
            new[0] = old[...]
        refs = refs[4:]
        refs = refs[:1] + tuple(r.at[1] for r in refs[1:5]) + refs[5:]
    both, other, back1, back2, back3, own, part0, part1, part2, part3 = refs
    backs = (own, back1, back2, back3)
    parts = (part0, part1, part2, part3)
    index = meta[0]
    blocks = (index, jnp.bitwise_xor(index, 1))
    group = index // STRIDE
    for h in range(HALF_HEADS):
        window = meta[2 + h]
        stride = meta[4 + h]
        q_rows, g_rows = [], []
        for half, (q_ref, g_ref) in enumerate(((q_mine, g_mine), (q_other, g_other))):
            for j in range(GROUP):
                at = slice((h * GROUP + j) * HEAD_DIM, (h * GROUP + j + 1) * HEAD_DIM)
                q_rows.append((q_ref[:, at].astype(jnp.float32) * gain[:, at]).astype(jnp.bfloat16))
                grad = g_ref[:, at]
                if has_head:
                    top = (h_mine, h_other)[half][:, at]
                    grad = jnp.where(meta[1] == 1, top, grad)
                g_rows.append(grad)
        q = jnp.concatenate(q_rows, axis=0)
        g = jnp.concatenate(g_rows, axis=0)
        k_at = slice(h * HEAD_DIM, (h + 1) * HEAD_DIM)
        v_at = slice(HALF_KV + h * HEAD_DIM, HALF_KV + (h + 1) * HEAD_DIM)
        k = jnp.concatenate([r[:, k_at] for r in pairs + strided], axis=0)
        v = jnp.concatenate([r[:, v_at] for r in pairs + strided], axis=0)
        scores = lax.dot_general(k, q, NT, preferred_element_type=jnp.float32)
        wide = GROUP * BLK
        key_row = lax.broadcasted_iota(jnp.int32, (BLK, wide), 0)
        query_row = lax.broadcasted_iota(jnp.int32, (BLK, wide), 1) % BLK
        rows = []
        for slot in range(12):
            cells = []
            for half in range(2):
                query_block = blocks[half]
                if slot < 8:
                    key_block = blocks[slot % 2] - 2 * (slot // 2)
                    gap = query_block - key_block
                    ok = (key_block >= 0) & (gap >= 0) & (gap < WIN)
                    ok = ok & ((gap < window) | (key_block % stride == 0))
                else:
                    key_block = STRIDE * (group - (slot - 8))
                    ok = (key_block >= 0) & (key_block <= query_block - WIN)
                    ok = ok & (key_block % stride == 0)
                cell = scores[slot * BLK : (slot + 1) * BLK, half * wide : (half + 1) * wide]
                if slot == half:
                    cell = jnp.where(key_row <= query_row, cell, NEG)
                else:
                    cell = jnp.where(ok, cell, NEG)
                cells.append(cell)
            rows.append(jnp.concatenate(cells, axis=1))
        scores = jnp.concatenate(rows, axis=0)
        peak = jnp.max(scores, axis=0, keepdims=True)
        weights = jnp.exp2((scores - peak) * (SCALE * LOG2E))
        probs = weights * (1.0 / jnp.sum(weights, axis=0, keepdims=True))
        grad_prob = lax.dot_general(v, g, NT, preferred_element_type=jnp.float32)
        delta = jnp.sum(probs * grad_prob, axis=0, keepdims=True)
        dscore = (probs * (grad_prob - delta)).astype(jnp.bfloat16)
        dquery = lax.dot_general(dscore, k, TN, preferred_element_type=jnp.float32) * SCALE
        dkey = jnp.dot(dscore, q, preferred_element_type=jnp.float32) * SCALE
        dvalue = jnp.dot(probs.astype(jnp.bfloat16), g, preferred_element_type=jnp.float32)
        for half in range(2):
            for j in range(GROUP):
                at = slice((h * GROUP + j) * HEAD_DIM, (h * GROUP + j + 1) * HEAD_DIM)
                row = (half * GROUP + j) * BLK
                grad = g[row : row + BLK].astype(jnp.float32)
                total = grad + gain[:, at] * dquery[row : row + BLK]
                total = total.astype(jnp.bfloat16)
                both[half, :, at] = total
                if half == 1:
                    other[:, at] = total
        for d in range(4):
            rows_at = slice(2 * BLK * d, 2 * BLK * (d + 1))
            backs[d][:, k_at] = dkey[rows_at].astype(backs[d].dtype)
            backs[d][:, v_at] = dvalue[rows_at].astype(backs[d].dtype)
        for s in range(4):
            rows_at = slice(8 * BLK + BLK * s, 8 * BLK + BLK * (s + 1))
            parts[s][:, k_at] = dkey[rows_at].astype(parts[s].dtype)
            parts[s][:, v_at] = dvalue[rows_at].astype(parts[s].dtype)


WHOLE = pl.BlockSpec(memory_space=pltpu.VMEM)
SCALAR = pl.BlockSpec(memory_space=pltpu.SMEM)
WIDE = 2 * HALF_KV


def shape(dims, dtype):
    return jax.ShapeDtypeStruct(dims, dtype)


def attention(tick, meta, gain, keep, recv, grads, pairs, strided, earlier):
    def at(lead, *rest):
        return pl.BlockSpec((None,) + rest, lambda n: (lead, 0, 0))

    args = [meta, gain, keep, recv]
    specs = [SCALAR, WHOLE, at(tick, BLK, HALF_FEAT), at(tick, BLK, HALF_FEAT)]
    if grads is None:
        args += [keep, recv]
        specs += [at(2, BLK, HALF_FEAT), at(2, BLK, HALF_FEAT)]
    else:
        args += [grads, grads, keep, recv]
        specs += [at(0, BLK, HALF_FEAT), at(1, BLK, HALF_FEAT)]
        specs += [at(3, BLK, HALF_FEAT), at(3, BLK, HALF_FEAT)]
    args += list(pairs) + list(strided)
    specs += [at(tick, 2 * BLK, WIDE)] * 4 + [at(tick, BLK, WIDE)] * 4
    bf16, f32 = jnp.bfloat16, jnp.float32
    out_shape = [shape((2, BLK, HALF_FEAT), bf16)]
    if earlier is None:
        out_shape += [shape((BLK, HALF_FEAT), bf16)] + [shape((2 * BLK, WIDE), bf16)] * 3
    else:
        args += earlier
        specs += [WHOLE] * 4
        out_shape += [shape((2, BLK, HALF_FEAT), bf16)] + [shape((2, 2 * BLK, WIDE), bf16)] * 3
    out_shape += [shape((2 * BLK, WIDE), f32), shape((BLK, WIDE), f32)]
    out_shape += [shape((BLK, WIDE), bf16)] * 3
    return pl.pallas_call(
        functools.partial(attention_kernel, grads is not None),
        out_shape=out_shape,
        grid=(1,),
        in_specs=specs,
        out_specs=[WHOLE] * len(out_shape),
        compiler_params=pltpu.CompilerParams(vmem_limit_bytes=32 << 20),
        cost_estimate=pl.CostEstimate(
            flops=2 * 5 * 2 * 512 * 768 * 128, bytes_accessed=4 << 20, transcendentals=2 * 512 * 768
        ),
        name="attention",
    )(*args)


def simple(kernel, out_shape, args, scalars=1):
    size = sum(a.size * a.dtype.itemsize for a in list(args) + list(out_shape))
    return pl.pallas_call(
        kernel,
        out_shape=out_shape,
        in_specs=[SCALAR] * scalars + [WHOLE] * (len(args) - scalars),
        out_specs=[WHOLE] * len(out_shape),
        compiler_params=pltpu.CompilerParams(vmem_limit_bytes=16 << 20),
        cost_estimate=pl.CostEstimate(flops=size, bytes_accessed=size, transcendentals=0),
        name=kernel.__name__,
    )(*args)


def column_sum(*refs):
    wide_out, send_out = refs[8:]
    for t in range(2):
        total = refs[4 * t][...]
        for s in range(1, 4):
            total = total + refs[4 * t + s][...].astype(jnp.float32)
        wide_out[t] = total
        send_out[t] = total.astype(jnp.bfloat16)


def split_keys(meta, keys, values, keep, give):
    swap = meta[0] % 2 == 1
    for source, at in ((keys, 0), (values, HALF_KV)):
        low, high = source[0, :, :, :HALF_KV], source[0, :, :, HALF_KV:]
        keep[:, :, at : at + HALF_KV] = jnp.where(swap, high, low)
        give[:, :, at : at + HALF_KV] = jnp.where(swap, low, high)


def split_rows(meta, inputs, first, head, keep, give):
    swap = meta[0] % 2 == 1
    for n, source in enumerate((inputs.at[0, 0], inputs.at[0, 1], first.at[0], head.at[0])):
        low, high = source[:, :HALF_FEAT], source[:, HALF_FEAT:]
        keep[n] = jnp.where(swap, high, low)
        give[n] = jnp.where(swap, low, high)


def pair_keys(meta, keep, recv, up_low, up_high, pair, start):
    core = meta[0] % 2
    even = (meta[0] // 8) % 2 == 0
    pair[:, :BLK] = keep[...]
    pair[:, BLK:] = recv[...]
    near = jnp.where(core == 0, keep[...], recv[...])
    above = jnp.where(core == 0, up_low[...], up_high[...])
    start[...] = jnp.where(even, near, above)


def row_sum(meta, *refs):
    total, x1, x2, x3, own0, own1, back1, back2, back3 = refs[:9]
    mine_out, other_out, strided_out = refs[9:]
    index = meta[0]
    owner = (index // 2) % 4 == 0
    even = (index // 8) % 2 == 0
    first = (owner & even & (index % 2 == 0)).astype(jnp.float32)
    second = (owner & even & (index % 2 == 1)).astype(jnp.float32)
    for t, own in enumerate((own0, own1)):
        strided = total[t]
        for x in (x1, x2, x3):
            strided = strided + x[t].astype(jnp.float32)
        strided_out[t] = strided.astype(jnp.bfloat16)
        near = own[...]
        for back in (back1, back2, back3):
            near = near + back[t].astype(jnp.float32)
        mine_out[t] = near[:BLK] + first * strided
        other_out[t] = (near[BLK:] + second * strided).astype(jnp.bfloat16)


def finish(meta, mine, other, low, high, keys_out, values_out):
    swap = meta[0] % 2 == 1
    for t in range(2):
        own = (mine[t] + low[t].astype(jnp.float32)).astype(jnp.bfloat16)
        far = (other[t].astype(jnp.float32) + high[t].astype(jnp.float32)).astype(jnp.bfloat16)
        left, right = jnp.where(swap, far, own), jnp.where(swap, own, far)
        for out, at in ((keys_out, 0), (values_out, HALF_KV)):
            out[0, t, :, :HALF_KV] = left[:, at : at + HALF_KV]
            out[0, t, :, HALF_KV:] = right[:, at : at + HALF_KV]


def join_rows(meta, mine0, mine1, other, out):
    swap = meta[0] % 2 == 1
    for t, mine in enumerate((mine0, mine1)):
        near, far = mine[0], other[t]
        out[0, t, :, :HALF_FEAT] = jnp.where(swap, far, near)
        out[0, t, :, HALF_FEAT:] = jnp.where(swap, near, far)


def body(inputs, saved_keys, saved_values, query_gain, first_grads, head_grads, window, stride):
    index = lax.axis_index("ctx")
    section = lax.axis_index("pp")
    last = lax.axis_size("pp") - 1
    core = index % 2
    place = (index // 2) % 4
    f32, bf16 = jnp.float32, jnp.bfloat16

    def ctx(array, move, when=lambda i: True):
        return route(array, "ctx", lambda i: move(i) if when(i) else None)

    spot = index.astype(jnp.int32).reshape(1)
    half = shape((2, BLK, WIDE), bf16)
    kv_keep, kv_give = simple(split_keys, [half, half], [spot, saved_keys, saved_values])
    kv_recv = sibling(kv_give)
    up_low = ctx(kv_keep, lambda i: i + 8, lambda i: i % STRIDE == 0)
    up_high = ctx(kv_give, lambda i: i + 9, lambda i: i % STRIDE == 0)
    pair, start = simple(
        pair_keys,
        [shape((2, 2 * BLK, WIDE), bf16), half],
        [spot, kv_keep, kv_recv, up_low, up_high],
    )
    chosen = start
    for d in range(1, 4):
        across = ctx(start, lambda i: i + 2 * d, lambda i: (i // 2) % 4 == 0)
        chosen = jnp.where(place == d, across, chosen)
    pairs = [pair] + [ctx(pair, lambda i: i + 2 * d) for d in range(1, 4)]
    strided = [chosen] + [ctx(chosen, lambda i: i + STRIDE * s) for s in range(1, 4)]

    four = shape((4, BLK, HALF_FEAT), bf16)
    keep, give = simple(split_rows, [four, four], [spot, inputs, first_grads, head_grads])
    recv = sibling(give)
    gain = jnp.where(core == 0, query_gain[:, :HALF_FEAT], query_gain[:, HALF_FEAT:])
    heads = jnp.where(core == 0, window[0, :2], window[0, 2:])
    steps = jnp.where(core == 0, stride[0, :2], stride[0, 2:])
    top = jnp.where(section == last, 1, 0)
    meta = jnp.concatenate([jnp.stack([index, top]).astype(jnp.int32), heads, steps])

    first = attention(0, meta, gain, keep, recv, None, pairs, strided, None)
    grads = route(first[0], "pp", lambda i: i - 1)
    second = attention(1, meta, gain, keep, recv, grads, pairs, strided, first[1:5])
    columns = []
    for outs in (first, second):
        columns.append(outs[6])
        columns += [ctx(outs[6 + s], lambda i: i - STRIDE * s) for s in range(1, 4)]
    backs = [ctx(second[1 + d], lambda i: i - 2 * d) for d in range(1, 4)]
    other_rows = sibling(second[1])

    wide = shape((2, BLK, WIDE), f32)
    total, send = simple(column_sum, [wide, half], columns, 0)
    rows = [ctx(send, lambda i: i - 2 * d, lambda i: (i // 2) % 4 == d) for d in range(1, 4)]
    mine, other, down = simple(
        row_sum, [wide, half, half], [spot, total] + rows + [first[5], second[5]] + backs
    )
    other = sibling(other)
    low = ctx(down, lambda i: i - 8, lambda i: i % STRIDE == 8)
    high = ctx(down, lambda i: i - 9, lambda i: i % STRIDE == 9)
    keys_shape = shape(saved_keys.shape, bf16)
    key_grads, value_grads = simple(finish, [keys_shape, keys_shape], [spot, mine, other, low, high])
    (grads_out,) = simple(
        join_rows, [shape(inputs.shape, bf16)], [spot, first[0], second[0], other_rows]
    )
    return grads_out, key_grads, value_grads


def solution(mesh):
    in_specs = (
        P("pp", None, "ctx", None),
        P("pp", None, "ctx", None),
        P("pp", None, "ctx", None),
        P("pp", None),
        P("pp", "ctx", None),
        P(None, "ctx", None),
        P("pp", None),
        P("pp", None),
    )
    out_specs = (P("pp", None, "ctx", None), P("pp", None, "ctx", None), P("pp", None, "ctx", None))
    return jax.shard_map(body, mesh=mesh, in_specs=in_specs, out_specs=out_specs, check_vma=False)
```

```python
import functools

import jax
import jax.numpy as jnp
from jax import lax
from jax.experimental import pallas as pl
from jax.experimental.pallas import tpu as pltpu
from jax.sharding import PartitionSpec as P

BLK = 64
WIN = 7
STRIDE = 16
HEAD_DIM = 128
GROUP = 4
HALF_HEADS = 2
HALF_KV = HALF_HEADS * HEAD_DIM
HALF_FEAT = HALF_HEADS * GROUP * HEAD_DIM
SCALE = HEAD_DIM**-0.5
TA = 3
TB = 2
LOG2E = 1.4426950408889634
NEG = -1e30
NT = (((1,), (1,)), ((), ()))
TN = (((0,), (0,)), ((), ()))


def route(array, axis, move):
    size = lax.axis_size(axis)
    pairs = [(i, move(i)) for i in range(size)]
    return lax.ppermute(array, axis, [(a, b) for a, b in pairs if b is not None and 0 <= b < size])


def sibling(array):
    return route(array, "ctx", lambda i: i ^ 1)


def attention_kernel(tick, meta, gain, keep, recv, *refs):
    if tick:
        grads, refs = refs[0], refs[1:]
    pairs, strided = refs[:4], refs[4:8]
    refs = refs[8:]
    if tick:
        for old, new in zip(refs[:7], refs[8:15]):
            new[0] = old[...]
        refs = refs[7:]
        refs = refs[:1] + tuple(r.at[1] for r in refs[1:8]) + refs[8:]
    both, other, back1, back2, back3, part1, part2, part3, own, part0 = refs
    backs = (own, back1, back2, back3)
    parts = (part0, part1, part2, part3)
    index = meta[0]
    blocks = (index, jnp.bitwise_xor(index, 1))
    group = index // STRIDE
    for h in range(HALF_HEADS):
        window = meta[2 + h]
        stride = meta[4 + h]
        q_rows, g_rows = [], []
        for half, source in enumerate((keep, recv)):
            for j in range(GROUP):
                near = slice(j * HEAD_DIM, (j + 1) * HEAD_DIM)
                at = slice((h * GROUP + j) * HEAD_DIM, (h * GROUP + j + 1) * HEAD_DIM)
                rows = source[2 + 2 * tick + h, :, near].astype(jnp.float32)
                q_rows.append((rows * gain[:, at]).astype(jnp.bfloat16))
                if tick:
                    top = source[8 + h, :, near]
                    g_rows.append(jnp.where(meta[1] == 1, top, grads[half, :, at]))
                else:
                    g_rows.append(source[6 + h, :, near])
        q = jnp.concatenate(q_rows, axis=0)
        g = jnp.concatenate(g_rows, axis=0)
        k_at = slice(h * HEAD_DIM, (h + 1) * HEAD_DIM)
        v_at = slice(HALF_KV + h * HEAD_DIM, HALF_KV + (h + 1) * HEAD_DIM)
        k = jnp.concatenate([r[:, k_at] for r in pairs + strided], axis=0)
        v = jnp.concatenate([r[:, v_at] for r in pairs + strided], axis=0)
        scores = lax.dot_general(k, q, NT, preferred_element_type=jnp.float32)
        wide = GROUP * BLK
        key_row = lax.broadcasted_iota(jnp.int32, (BLK, wide), 0)
        query_row = lax.broadcasted_iota(jnp.int32, (BLK, wide), 1) % BLK
        rows = []
        for slot in range(12):
            cells = []
            for half in range(2):
                query_block = blocks[half]
                if slot < 8:
                    key_block = blocks[slot % 2] - 2 * (slot // 2)
                    gap = query_block - key_block
                    ok = (key_block >= 0) & (gap >= 0) & (gap < WIN)
                    ok = ok & ((gap < window) | (key_block % stride == 0))
                else:
                    key_block = STRIDE * (group - (slot - 8))
                    ok = (key_block >= 0) & (key_block <= query_block - WIN)
                    ok = ok & (key_block % stride == 0)
                cell = scores[slot * BLK : (slot + 1) * BLK, half * wide : (half + 1) * wide]
                if slot == half:
                    cell = jnp.where(key_row <= query_row, cell, NEG)
                else:
                    cell = jnp.where(ok, cell, NEG)
                cells.append(cell)
            rows.append(jnp.concatenate(cells, axis=1))
        scores = jnp.concatenate(rows, axis=0)
        peak = jnp.max(scores, axis=0, keepdims=True)
        weights = jnp.exp2((scores - peak) * (SCALE * LOG2E))
        probs = weights * (1.0 / jnp.sum(weights, axis=0, keepdims=True))
        grad_prob = lax.dot_general(v, g, NT, preferred_element_type=jnp.float32)
        delta = jnp.sum(probs * grad_prob, axis=0, keepdims=True)
        dscore = (probs * (grad_prob - delta)).astype(jnp.bfloat16)
        dquery = lax.dot_general(dscore, k, TN, preferred_element_type=jnp.float32) * SCALE
        dkey = jnp.dot(dscore, q, preferred_element_type=jnp.float32) * SCALE
        dvalue = jnp.dot(probs.astype(jnp.bfloat16), g, preferred_element_type=jnp.float32)
        for half in range(2):
            for j in range(GROUP):
                at = slice((h * GROUP + j) * HEAD_DIM, (h * GROUP + j + 1) * HEAD_DIM)
                row = (half * GROUP + j) * BLK
                grad = g[row : row + BLK].astype(jnp.float32)
                total = grad + gain[:, at] * dquery[row : row + BLK]
                total = total.astype(jnp.bfloat16)
                both[half, :, at] = total
                if half == 1:
                    other[:, at] = total
        for d in range(4):
            rows_at = slice(2 * BLK * d, 2 * BLK * (d + 1))
            backs[d][:, k_at] = dkey[rows_at].astype(backs[d].dtype)
            backs[d][:, v_at] = dvalue[rows_at].astype(backs[d].dtype)
        for s in range(4):
            rows_at = slice(8 * BLK + BLK * s, 8 * BLK + BLK * (s + 1))
            parts[s][:, k_at] = dkey[rows_at].astype(parts[s].dtype)
            parts[s][:, v_at] = dvalue[rows_at].astype(parts[s].dtype)


WHOLE = pl.BlockSpec(memory_space=pltpu.VMEM)
SCALAR = pl.BlockSpec(memory_space=pltpu.SMEM)
WIDE = 2 * HALF_KV


def shape(dims, dtype):
    return jax.ShapeDtypeStruct(dims, dtype)


def attention(tick, meta, gain, keep, recv, grads, pairs, strided, earlier):
    def at(lead, *rest):
        return pl.BlockSpec((None,) + rest, lambda n: (lead, 0, 0))

    args = [meta, gain, keep, recv]
    specs = [SCALAR, WHOLE, WHOLE, WHOLE]
    if tick:
        args.append(grads)
        specs.append(WHOLE)
    args += list(pairs) + list(strided)
    specs += [at(tick, 2 * BLK, WIDE)] * 4 + [at(tick, BLK, WIDE)] * 4
    bf16, f32 = jnp.bfloat16, jnp.float32
    out_shape = [shape((2, BLK, HALF_FEAT), bf16)]
    lead = (2,) if tick else ()
    if tick:
        args += earlier
        specs += [WHOLE] * 7
    out_shape.append(shape(lead + (BLK, HALF_FEAT), bf16))
    out_shape += [shape(lead + (2 * BLK, WIDE), bf16)] * 3
    out_shape += [shape(lead + (BLK, WIDE), bf16)] * 3
    out_shape += [shape((2 * BLK, WIDE), f32), shape((BLK, WIDE), f32)]
    return pl.pallas_call(
        functools.partial(attention_kernel, tick),
        out_shape=out_shape,
        grid=(1,),
        in_specs=specs,
        out_specs=[WHOLE] * len(out_shape),
        compiler_params=pltpu.CompilerParams(vmem_limit_bytes=32 << 20),
        cost_estimate=pl.CostEstimate(
            flops=2 * 5 * 2 * 512 * 768 * 128, bytes_accessed=4 << 20, transcendentals=2 * 512 * 768
        ),
        name="attention",
    )(*args)


def simple(kernel, out_shape, args, scalars=1):
    size = sum(a.size * a.dtype.itemsize for a in list(args) + list(out_shape))
    return pl.pallas_call(
        kernel,
        out_shape=out_shape,
        in_specs=[SCALAR] * scalars + [WHOLE] * (len(args) - scalars),
        out_specs=[WHOLE] * len(out_shape),
        compiler_params=pltpu.CompilerParams(vmem_limit_bytes=16 << 20),
        cost_estimate=pl.CostEstimate(flops=size, bytes_accessed=size, transcendentals=0),
        name=kernel.__name__,
    )(*args)


def column_sum(own0, own1, x1, x2, x3, wide_out, send_out):
    for t, own in enumerate((own0, own1)):
        total = own[...]
        for x in (x1, x2, x3):
            total = total + x[t].astype(jnp.float32)
        wide_out[t] = total
        send_out[t] = total.astype(jnp.bfloat16)


def split_all(meta, keys, values, inputs, first, head, keep, give, kv_keep, kv_give):
    swap = meta[0] % 2 == 1
    for source, at in ((keys, 0), (values, HALF_KV)):
        low, high = source[0, :, :, :HALF_KV], source[0, :, :, HALF_KV:]
        mine, far = jnp.where(swap, high, low), jnp.where(swap, low, high)
        keep[:2, :, at : at + HALF_KV] = mine
        give[:2, :, at : at + HALF_KV] = far
        kv_keep[:, :, at : at + HALF_KV] = mine
        kv_give[:, :, at : at + HALF_KV] = far
    for n, source in enumerate((inputs.at[0, 0], inputs.at[0, 1], first.at[0], head.at[0])):
        for h in range(HALF_HEADS):
            low = source[:, h * WIDE : (h + 1) * WIDE]
            high = source[:, HALF_FEAT + h * WIDE : HALF_FEAT + (h + 1) * WIDE]
            keep[2 + 2 * n + h] = jnp.where(swap, high, low)
            give[2 + 2 * n + h] = jnp.where(swap, low, high)


def pair_keys(meta, keep, recv, up_low, up_high, pair, start):
    keep, recv = keep.at[:2], recv.at[:2]
    core = meta[0] % 2
    even = (meta[0] // 8) % 2 == 0
    pair[:, :BLK] = keep[...]
    pair[:, BLK:] = recv[...]
    near = jnp.where(core == 0, keep[...], recv[...])
    above = jnp.where(core == 0, up_low[...], up_high[...])
    start[...] = jnp.where(even, near, above)


def choose(meta, start, x1, x2, x3, out):
    place = (meta[0] // 2) % 4
    near = jnp.where(place == 0, start[...], x1[...])
    far = jnp.where(place == 2, x2[...], x3[...])
    out[...] = jnp.where(place < 2, near, far)


def row_sum(meta, *refs):
    total, x1, x2, x3, own0, own1, back1, back2, back3, far_rows = refs[:10]
    mine_out, swap_out, strided_out = refs[10:]
    index = meta[0]
    owner = (index // 2) % 4 == 0
    even = (index // 8) % 2 == 0
    first = (owner & even & (index % 2 == 0)).astype(jnp.float32)
    second = (owner & even & (index % 2 == 1)).astype(jnp.float32)
    for t, own in enumerate((own0, own1)):
        strided = total[t]
        for x in (x1, x2, x3):
            strided = strided + x[t].astype(jnp.float32)
        strided_out[t] = strided.astype(jnp.bfloat16)
        near = own[...]
        for back in (back1, back2, back3):
            near = near + back[t].astype(jnp.float32)
        mine_out[t] = near[:BLK] + first * strided
        swap_out[t, :, :HALF_FEAT] = far_rows[t]
        swap_out[t, :, HALF_FEAT:] = (near[BLK:] + second * strided).astype(jnp.bfloat16)


def finish(meta, mine, swapped, low, high, mine0, mine1, rows_out, keys_out, values_out):
    swap = meta[0] % 2 == 1
    for t, rows in enumerate((mine0, mine1)):
        other = swapped[t, :, HALF_FEAT:].astype(jnp.float32)
        own = (mine[t] + low[t].astype(jnp.float32)).astype(jnp.bfloat16)
        far = (other + high[t].astype(jnp.float32)).astype(jnp.bfloat16)
        left, right = jnp.where(swap, far, own), jnp.where(swap, own, far)
        for out, at in ((keys_out, 0), (values_out, HALF_KV)):
            out[0, t, :, :HALF_KV] = left[:, at : at + HALF_KV]
            out[0, t, :, HALF_KV:] = right[:, at : at + HALF_KV]
        near, far = rows[0], swapped[t, :, :HALF_FEAT]
        rows_out[0, t, :, :HALF_FEAT] = jnp.where(swap, far, near)
        rows_out[0, t, :, HALF_FEAT:] = jnp.where(swap, near, far)


def body(inputs, saved_keys, saved_values, query_gain, first_grads, head_grads, window, stride):
    index = lax.axis_index("ctx")
    section = lax.axis_index("pp")
    last = lax.axis_size("pp") - 1
    core = index % 2
    place = (index // 2) % 4
    f32, bf16 = jnp.float32, jnp.bfloat16

    def ctx(array, move, when=lambda i: True):
        return route(array, "ctx", lambda i: move(i) if when(i) else None)

    spot = index.astype(jnp.int32).reshape(1)
    half = shape((2, BLK, WIDE), bf16)
    ten = shape((10, BLK, WIDE), bf16)
    keep, give, kv_keep, kv_give = simple(
        split_all,
        [ten, ten, half, half],
        [spot, saved_keys, saved_values, inputs, first_grads, head_grads],
    )
    recv = sibling(give)
    up_low = ctx(kv_keep, lambda i: i + 8, lambda i: i % STRIDE == 0)
    up_high = ctx(kv_give, lambda i: i + 9, lambda i: i % STRIDE == 0)
    pair, start = simple(
        pair_keys,
        [shape((2, 2 * BLK, WIDE), bf16), half],
        [spot, keep, recv, up_low, up_high],
    )
    across = [ctx(start, lambda i: i + 2 * d, lambda i: (i // 2) % 4 == 0) for d in range(1, 4)]
    (chosen,) = simple(choose, [half], [spot, start] + across)
    pairs = [pair] + [ctx(pair, lambda i: i + 2 * d) for d in range(1, 4)]
    strided = [chosen]
    for s in range(1, 4):
        sent = chosen
        if s == 1:
            sent, pairs[TA] = lax.optimization_barrier((chosen, pairs[TA]))
        strided.append(ctx(sent, lambda i: i + STRIDE * s))

    gain = jnp.where(core == 0, query_gain[:, :HALF_FEAT], query_gain[:, HALF_FEAT:])
    heads = jnp.where(core == 0, window[0, :2], window[0, 2:])
    steps = jnp.where(core == 0, stride[0, :2], stride[0, 2:])
    top = jnp.where(section == last, 1, 0)
    meta = jnp.concatenate([jnp.stack([index, top]).astype(jnp.int32), heads, steps])

    first = attention(0, meta, gain, keep, recv, None, pairs, strided, None)
    grads = route(first[0], "pp", lambda i: i - 1)
    second = attention(1, meta, gain, keep, recv, grads, pairs, strided, first[1:8])
    columns = [first[9], second[9]]
    columns += [ctx(second[4 + s], lambda i: i - STRIDE * s) for s in range(1, 4)]
    backs = [ctx(second[1 + d], lambda i: i - 2 * d) for d in range(1, 4)]

    wide = shape((2, BLK, WIDE), f32)
    total, send = simple(column_sum, [wide, half], columns, 0)
    rows = []
    for d in range(1, 4):
        sent = send
        if d == 1:
            sent, backs[TB] = lax.optimization_barrier((send, backs[TB]))
        rows.append(ctx(sent, lambda i: i - 2 * d, lambda i: (i // 2) % 4 == d))
    mine, swap, down = simple(
        row_sum,
        [wide, shape((2, BLK, HALF_FEAT + WIDE), bf16), half],
        [spot, total] + rows + [first[8], second[8]] + backs + [second[1]],
    )
    swapped = sibling(swap)
    low = ctx(down, lambda i: i - 8, lambda i: i % STRIDE == 8)
    high = ctx(down, lambda i: i - 9, lambda i: i % STRIDE == 9)
    keys_shape = shape(saved_keys.shape, bf16)
    grads_out, key_grads, value_grads = simple(
        finish,
        [shape(inputs.shape, bf16), keys_shape, keys_shape],
        [spot, mine, swapped, low, high, first[0], second[0]],
    )
    return grads_out, key_grads, value_grads


def solution(mesh):
    in_specs = (
        P("pp", None, "ctx", None),
        P("pp", None, "ctx", None),
        P("pp", None, "ctx", None),
        P("pp", None),
        P("pp", "ctx", None),
        P(None, "ctx", None),
        P("pp", None),
        P("pp", None),
    )
    out_specs = (P("pp", None, "ctx", None), P("pp", None, "ctx", None), P("pp", None, "ctx", None))
    return jax.shard_map(body, mesh=mesh, in_specs=in_specs, out_specs=out_specs, check_vma=False)
```

```python
import functools

import jax
import jax.numpy as jnp
from jax import lax
from jax.experimental import pallas as pl
from jax.experimental.pallas import tpu as pltpu
from jax.sharding import PartitionSpec as P

BLK = 64
WIN = 7
STRIDE = 16
HEAD_DIM = 128
GROUP = 4
HALF_HEADS = 2
HALF_KV = HALF_HEADS * HEAD_DIM
HALF_FEAT = HALF_HEADS * GROUP * HEAD_DIM
SCALE = HEAD_DIM**-0.5
LOG2E = 1.4426950408889634
NEG = -1e30
NT = (((1,), (1,)), ((), ()))
TN = (((0,), (0,)), ((), ()))


def route(array, axis, move):
    size = lax.axis_size(axis)
    pairs = [(i, move(i)) for i in range(size)]
    return lax.ppermute(array, axis, [(a, b) for a, b in pairs if b is not None and 0 <= b < size])


def sibling(array):
    return route(array, "ctx", lambda i: i ^ 1)


def attention_kernel(tick, meta, gain, keep, recv, *refs):
    if tick:
        grads, refs = refs[0], refs[1:]
    pairs, strided = refs[:4], refs[4:8]
    refs = refs[8:]
    if tick:
        for old, new in zip(refs[:4], refs[6:10]):
            new[0] = old[...]
        refs[10][:, 0] = refs[4][...]
        refs = refs[5:]
        refs = refs[:1] + tuple(r.at[1] for r in refs[1:5]) + refs[5:]
    both, other, back1, back2, back3, parts, own = refs
    backs = (own, back1, back2, back3)
    index = meta[0]
    blocks = (index, jnp.bitwise_xor(index, 1))
    group = index // STRIDE
    for h in range(HALF_HEADS):
        window = meta[2 + h]
        stride = meta[4 + h]
        q_rows, g_rows = [], []
        for half, source in enumerate((keep, recv)):
            for j in range(GROUP):
                near = slice(j * HEAD_DIM, (j + 1) * HEAD_DIM)
                at = slice((h * GROUP + j) * HEAD_DIM, (h * GROUP + j + 1) * HEAD_DIM)
                rows = source[2 + 2 * tick + h, :, near].astype(jnp.float32)
                q_rows.append((rows * gain[:, at]).astype(jnp.bfloat16))
                if tick:
                    top = source[8 + h, :, near]
                    g_rows.append(jnp.where(meta[1] == 1, top, grads[half, :, at]))
                else:
                    g_rows.append(source[6 + h, :, near])
        q = jnp.concatenate(q_rows, axis=0)
        g = jnp.concatenate(g_rows, axis=0)
        k_at = slice(h * HEAD_DIM, (h + 1) * HEAD_DIM)
        v_at = slice(HALF_KV + h * HEAD_DIM, HALF_KV + (h + 1) * HEAD_DIM)
        k = jnp.concatenate([r[:, k_at] for r in pairs + strided], axis=0)
        v = jnp.concatenate([r[:, v_at] for r in pairs + strided], axis=0)
        scores = lax.dot_general(k, q, NT, preferred_element_type=jnp.float32)
        wide = GROUP * BLK
        key_row = lax.broadcasted_iota(jnp.int32, (BLK, wide), 0)
        query_row = lax.broadcasted_iota(jnp.int32, (BLK, wide), 1) % BLK
        rows = []
        for slot in range(12):
            cells = []
            for half in range(2):
                query_block = blocks[half]
                if slot < 8:
                    key_block = blocks[slot % 2] - 2 * (slot // 2)
                    gap = query_block - key_block
                    ok = (key_block >= 0) & (gap >= 0) & (gap < WIN)
                    ok = ok & ((gap < window) | (key_block % stride == 0))
                else:
                    key_block = STRIDE * (group - (slot - 8))
                    ok = (key_block >= 0) & (key_block <= query_block - WIN)
                    ok = ok & (key_block % stride == 0)
                cell = scores[slot * BLK : (slot + 1) * BLK, half * wide : (half + 1) * wide]
                if slot == half:
                    cell = jnp.where(key_row <= query_row, cell, NEG)
                else:
                    cell = jnp.where(ok, cell, NEG)
                cells.append(cell)
            rows.append(jnp.concatenate(cells, axis=1))
        scores = jnp.concatenate(rows, axis=0)
        peak = jnp.max(scores, axis=0, keepdims=True)
        weights = jnp.exp2((scores - peak) * (SCALE * LOG2E))
        probs = weights * (1.0 / jnp.sum(weights, axis=0, keepdims=True))
        grad_prob = lax.dot_general(v, g, NT, preferred_element_type=jnp.float32)
        delta = jnp.sum(probs * grad_prob, axis=0, keepdims=True)
        dscore = (probs * (grad_prob - delta)).astype(jnp.bfloat16)
        dquery = lax.dot_general(dscore, k, TN, preferred_element_type=jnp.float32) * SCALE
        dkey = jnp.dot(dscore, q, preferred_element_type=jnp.float32) * SCALE
        dvalue = jnp.dot(probs.astype(jnp.bfloat16), g, preferred_element_type=jnp.float32)
        for half in range(2):
            for j in range(GROUP):
                at = slice((h * GROUP + j) * HEAD_DIM, (h * GROUP + j + 1) * HEAD_DIM)
                row = (half * GROUP + j) * BLK
                grad = g[row : row + BLK].astype(jnp.float32)
                total = grad + gain[:, at] * dquery[row : row + BLK]
                total = total.astype(jnp.bfloat16)
                both[half, :, at] = total
                if half == 1:
                    other[:, at] = total
        for d in range(4):
            rows_at = slice(2 * BLK * d, 2 * BLK * (d + 1))
            backs[d][:, k_at] = dkey[rows_at].astype(backs[d].dtype)
            backs[d][:, v_at] = dvalue[rows_at].astype(backs[d].dtype)
        for s in range(4):
            rows_at = slice(8 * BLK + BLK * s, 8 * BLK + BLK * (s + 1))
            spot = jnp.bitwise_and(group - s, 3)
            part = parts.at[spot, 1] if tick else parts.at[spot]
            part[:, k_at] = dkey[rows_at].astype(jnp.bfloat16)
            part[:, v_at] = dvalue[rows_at].astype(jnp.bfloat16)


WHOLE = pl.BlockSpec(memory_space=pltpu.VMEM)
SCALAR = pl.BlockSpec(memory_space=pltpu.SMEM)
WIDE = 2 * HALF_KV


def shape(dims, dtype):
    return jax.ShapeDtypeStruct(dims, dtype)


def attention(tick, meta, gain, keep, recv, grads, pairs, strided, earlier):
    def at(lead, *rest):
        return pl.BlockSpec((None,) + rest, lambda n: (lead, 0, 0))

    args = [meta, gain, keep, recv]
    specs = [SCALAR, WHOLE, WHOLE, WHOLE]
    if tick:
        args.append(grads)
        specs.append(WHOLE)
    args += list(pairs) + list(strided)
    specs += [at(tick, 2 * BLK, WIDE)] * 4 + [WHOLE] * 4
    bf16, f32 = jnp.bfloat16, jnp.float32
    out_shape = [shape((2, BLK, HALF_FEAT), bf16)]
    lead = (2,) if tick else ()
    if tick:
        args += earlier
        specs += [WHOLE] * 5
    out_shape.append(shape(lead + (BLK, HALF_FEAT), bf16))
    out_shape += [shape(lead + (2 * BLK, WIDE), bf16)] * 3
    out_shape.append(shape((4,) + lead + (BLK, WIDE), bf16))
    out_shape.append(shape((2 * BLK, WIDE), f32))
    return pl.pallas_call(
        functools.partial(attention_kernel, tick),
        out_shape=out_shape,
        grid=(1,),
        in_specs=specs,
        out_specs=[WHOLE] * len(out_shape),
        compiler_params=pltpu.CompilerParams(vmem_limit_bytes=32 << 20),
        cost_estimate=pl.CostEstimate(
            flops=2 * 5 * 2 * 512 * 768 * 128, bytes_accessed=4 << 20, transcendentals=2 * 512 * 768
        ),
        name="attention",
    )(*args)


def simple(kernel, out_shape, args, blocked=False):
    size = sum(a.size * a.dtype.itemsize for a in list(args) + list(out_shape))

    def all_of(array):
        return pl.BlockSpec(array.shape, lambda n: (0,) * array.ndim)

    return pl.pallas_call(
        kernel,
        out_shape=out_shape,
        grid=(1,),
        in_specs=[SCALAR] + [all_of(a) if blocked else WHOLE for a in args[1:]],
        out_specs=[WHOLE] * len(out_shape),
        compiler_params=pltpu.CompilerParams(vmem_limit_bytes=16 << 20),
        cost_estimate=pl.CostEstimate(flops=size, bytes_accessed=size, transcendentals=0),
        name=kernel.__name__,
    )(*args)


def split_all(meta, keys, values, inputs, first, head, keep, give, kv_keep, kv_give):
    swap = meta[0] % 2 == 1
    for source, at in ((keys, 0), (values, HALF_KV)):
        low, high = source[0, :, :, :HALF_KV], source[0, :, :, HALF_KV:]
        mine, far = jnp.where(swap, high, low), jnp.where(swap, low, high)
        keep[:2, :, at : at + HALF_KV] = mine
        give[:2, :, at : at + HALF_KV] = far
        kv_keep[:, :, at : at + HALF_KV] = mine
        kv_give[:, :, at : at + HALF_KV] = far
    for n, source in enumerate((inputs.at[0, 0], inputs.at[0, 1], first.at[0], head.at[0])):
        for h in range(HALF_HEADS):
            low = source[:, h * WIDE : (h + 1) * WIDE]
            high = source[:, HALF_FEAT + h * WIDE : HALF_FEAT + (h + 1) * WIDE]
            keep[2 + 2 * n + h] = jnp.where(swap, high, low)
            give[2 + 2 * n + h] = jnp.where(swap, low, high)


def pair_keys(meta, keep, recv, up_low, up_high, pair, start):
    keep, recv = keep.at[:2], recv.at[:2]
    core = meta[0] % 2
    even = (meta[0] // 8) % 2 == 0
    pair[:, :BLK] = keep[...]
    pair[:, BLK:] = recv[...]
    near = jnp.where(core == 0, keep[...], recv[...])
    above = jnp.where(core == 0, up_low[...], up_high[...])
    start[...] = jnp.where(even, near, above)


def choose(meta, start, x1, x2, x3, *outs):
    place = (meta[0] // 2) % 4
    for t, out in enumerate(outs):
        near = jnp.where(place == 0, start[t], x1[t])
        far = jnp.where(place == 2, x2[t], x3[t])
        out[...] = jnp.where(place < 2, near, far)


def fold(meta, pieces, own0, own1, back1, back2, back3, far_rows, sums, mine, swap):
    total = pieces[0].astype(jnp.float32)
    for n in range(1, 32):
        total = total + pieces[n].astype(jnp.float32)
    total = total.astype(jnp.bfloat16)
    for n in range(STRIDE):
        sums[n] = total
    for t, own in enumerate((own0, own1)):
        near = own[...]
        for back in (back1, back2, back3):
            near = near + back[t].astype(jnp.float32)
        mine[t] = near[:BLK]
        swap[t, :, :HALF_FEAT] = far_rows[t]
        swap[t, :, HALF_FEAT:] = near[BLK:].astype(jnp.bfloat16)


def finish(meta, mine, swapped, sums, mine0, mine1, rows_out, keys_out, values_out):
    swap = meta[0] % 2 == 1
    owner = meta[0] % STRIDE == 0
    for t, rows in enumerate((mine0, mine1)):
        strided = []
        for half in range(2):
            quarters = [sums[2 * (4 * t + n) + half] for n in range(4)]
            whole = jnp.concatenate(quarters, axis=0).astype(jnp.float32)
            strided.append(jnp.where(owner, whole, 0.0))
        own = (mine[t] + strided[0]).astype(jnp.bfloat16)
        far = (swapped[t, :, HALF_FEAT:].astype(jnp.float32) + strided[1]).astype(jnp.bfloat16)
        left, right = jnp.where(swap, far, own), jnp.where(swap, own, far)
        for out, at in ((keys_out, 0), (values_out, HALF_KV)):
            out[0, t, :, :HALF_KV] = left[:, at : at + HALF_KV]
            out[0, t, :, HALF_KV:] = right[:, at : at + HALF_KV]
        near, far = rows[0], swapped[t, :, :HALF_FEAT]
        rows_out[0, t, :, :HALF_FEAT] = jnp.where(swap, far, near)
        rows_out[0, t, :, HALF_FEAT:] = jnp.where(swap, near, far)


def body(inputs, saved_keys, saved_values, query_gain, first_grads, head_grads, window, stride):
    index = lax.axis_index("ctx")
    section = lax.axis_index("pp")
    last = lax.axis_size("pp") - 1
    core = index % 2
    place = (index // 2) % 4
    f32, bf16 = jnp.float32, jnp.bfloat16

    def ctx(array, move, when=lambda i: True):
        return route(array, "ctx", lambda i: move(i) if when(i) else None)

    spot = index.astype(jnp.int32).reshape(1)
    half = shape((2, BLK, WIDE), bf16)
    ten = shape((10, BLK, WIDE), bf16)
    keep, give, kv_keep, kv_give = simple(
        split_all,
        [ten, ten, half, half],
        [spot, saved_keys, saved_values, inputs, first_grads, head_grads],
        blocked=True,
    )
    recv = sibling(give)
    up_low = ctx(kv_keep, lambda i: i + 8, lambda i: i % STRIDE == 0)
    up_high = ctx(kv_give, lambda i: i + 9, lambda i: i % STRIDE == 0)
    pair, start = simple(
        pair_keys,
        [shape((2, 2 * BLK, WIDE), bf16), half],
        [spot, keep, recv, up_low, up_high],
    )
    across = [ctx(start, lambda i: i + 2 * d, lambda i: (i // 2) % 4 == 0) for d in range(1, 4)]
    chosen = simple(choose, [shape((BLK, WIDE), bf16)] * 2, [spot, start] + across)
    pairs = [pair] + [ctx(pair, lambda i: i + 2 * d) for d in range(1, 4)]

    def columns(block):
        return [ctx(block, lambda i: i + STRIDE * s) for s in range(1, 4)]

    gain = jnp.where(core == 0, query_gain[:, :HALF_FEAT], query_gain[:, HALF_FEAT:])
    heads = jnp.where(core == 0, window[0, :2], window[0, 2:])
    steps = jnp.where(core == 0, stride[0, :2], stride[0, 2:])
    top = jnp.where(section == last, 1, 0)
    meta = jnp.concatenate([jnp.stack([index, top]).astype(jnp.int32), heads, steps])

    strided = [chosen[0]] + columns(chosen[0])
    first = attention(0, meta, gain, keep, recv, None, pairs, strided, None)
    grads = route(first[0], "pp", lambda i: i - 1)
    late, own = lax.optimization_barrier((chosen[1], first[6]))
    strided = [late] + columns(late)
    second = attention(1, meta, gain, keep, recv, grads, pairs, strided, first[1:6])
    backs = [ctx(second[1 + d], lambda i: i - 2 * d) for d in range(1, 4)]
    size = lax.axis_size("ctx")
    teams = [[2 * n + k for n in range(size // 2)] for k in range(2)]
    pieces = second[5].reshape(32, 16, WIDE)
    pieces = lax.all_to_all(pieces, "ctx", 0, 0, tiled=True, axis_index_groups=teams)
    sums, mine, swap = simple(
        fold,
        [
            shape((STRIDE, 16, WIDE), bf16),
            shape((2, BLK, WIDE), f32),
            shape((2, BLK, HALF_FEAT + WIDE), bf16),
        ],
        [spot, pieces, own, second[6]] + backs + [second[1]],
    )
    swapped = sibling(swap)
    groups = [[STRIDE * k + n for n in range(STRIDE)] for k in range(size // STRIDE)]
    sums = lax.all_to_all(sums, "ctx", 0, 0, tiled=True, axis_index_groups=groups)
    keys_shape = shape(saved_keys.shape, bf16)
    grads_out, key_grads, value_grads = simple(
        finish,
        [shape(inputs.shape, bf16), keys_shape, keys_shape],
        [spot, mine, swapped, sums, first[0], second[0]],
    )
    return grads_out, key_grads, value_grads


def solution(mesh):
    in_specs = (
        P("pp", None, "ctx", None),
        P("pp", None, "ctx", None),
        P("pp", None, "ctx", None),
        P("pp", None),
        P("pp", "ctx", None),
        P(None, "ctx", None),
        P("pp", None),
        P("pp", None),
    )
    out_specs = (P("pp", None, "ctx", None), P("pp", None, "ctx", None), P("pp", None, "ctx", None))
    return jax.shard_map(body, mesh=mesh, in_specs=in_specs, out_specs=out_specs, check_vma=False)
```

```python
import functools

import jax
import jax.numpy as jnp
from jax import lax
from jax.experimental import pallas as pl
from jax.experimental.pallas import tpu as pltpu
from jax.sharding import PartitionSpec as P

BLK = 64
WIN = 7
STRIDE = 16
HEAD_DIM = 128
GROUP = 4
HALF_HEADS = 2
HALF_KV = HALF_HEADS * HEAD_DIM
HALF_FEAT = HALF_HEADS * GROUP * HEAD_DIM
SCALE = HEAD_DIM**-0.5
TA = 3
LOG2E = 1.4426950408889634
NEG = -1e30
NT = (((1,), (1,)), ((), ()))
TN = (((0,), (0,)), ((), ()))


def route(array, axis, move):
    size = lax.axis_size(axis)
    pairs = [(i, move(i)) for i in range(size)]
    return lax.ppermute(array, axis, [(a, b) for a, b in pairs if b is not None and 0 <= b < size])


def sibling(array):
    return route(array, "ctx", lambda i: i ^ 1)


def attention_kernel(tick, meta, gain, keep, recv, *refs):
    if tick:
        grads, refs = refs[0], refs[1:]
    pairs, strided = refs[:4], refs[4:8]
    refs = refs[8:]
    if tick:
        for old, new in zip(refs[:4], refs[5:9]):
            new[0] = old[...]
        refs = refs[4:]
        refs = refs[:1] + tuple(r.at[1] for r in refs[1:5]) + refs[5:]
    both, other, back1, back2, back3, own, part0, part1, part2, part3 = refs
    backs = (own, back1, back2, back3)
    parts = (part0, part1, part2, part3)
    index = meta[0]
    blocks = (index, jnp.bitwise_xor(index, 1))
    group = index // STRIDE
    for h in range(HALF_HEADS):
        window = meta[2 + h]
        stride = meta[4 + h]
        q_rows, g_rows = [], []
        for half, source in enumerate((keep, recv)):
            for j in range(GROUP):
                near = slice(j * HEAD_DIM, (j + 1) * HEAD_DIM)
                at = slice((h * GROUP + j) * HEAD_DIM, (h * GROUP + j + 1) * HEAD_DIM)
                rows = source[2 + 2 * tick + h, :, near].astype(jnp.float32)
                q_rows.append((rows * gain[:, at]).astype(jnp.bfloat16))
                if tick:
                    top = source[8 + h, :, near]
                    g_rows.append(jnp.where(meta[1] == 1, top, grads[half, :, at]))
                else:
                    g_rows.append(source[6 + h, :, near])
        q = jnp.concatenate(q_rows, axis=0)
        g = jnp.concatenate(g_rows, axis=0)
        k_at = slice(h * HEAD_DIM, (h + 1) * HEAD_DIM)
        v_at = slice(HALF_KV + h * HEAD_DIM, HALF_KV + (h + 1) * HEAD_DIM)
        k = jnp.concatenate([r[:, k_at] for r in pairs + strided], axis=0)
        v = jnp.concatenate([r[:, v_at] for r in pairs + strided], axis=0)
        scores = lax.dot_general(k, q, NT, preferred_element_type=jnp.float32)
        wide = GROUP * BLK
        key_row = lax.broadcasted_iota(jnp.int32, (BLK, wide), 0)
        query_row = lax.broadcasted_iota(jnp.int32, (BLK, wide), 1) % BLK
        rows = []
        for slot in range(12):
            cells = []
            for half in range(2):
                query_block = blocks[half]
                if slot < 8:
                    key_block = blocks[slot % 2] - 2 * (slot // 2)
                    gap = query_block - key_block
                    ok = (key_block >= 0) & (gap >= 0) & (gap < WIN)
                    ok = ok & ((gap < window) | (key_block % stride == 0))
                else:
                    key_block = STRIDE * (group - (slot - 8))
                    ok = (key_block >= 0) & (key_block <= query_block - WIN)
                    ok = ok & (key_block % stride == 0)
                cell = scores[slot * BLK : (slot + 1) * BLK, half * wide : (half + 1) * wide]
                if slot == half:
                    cell = jnp.where(key_row <= query_row, cell, NEG)
                else:
                    cell = jnp.where(ok, cell, NEG)
                cells.append(cell)
            rows.append(jnp.concatenate(cells, axis=1))
        scores = jnp.concatenate(rows, axis=0)
        peak = jnp.max(scores, axis=0, keepdims=True)
        weights = jnp.exp2((scores - peak) * (SCALE * LOG2E))
        probs = weights * (1.0 / jnp.sum(weights, axis=0, keepdims=True))
        grad_prob = lax.dot_general(v, g, NT, preferred_element_type=jnp.float32)
        delta = jnp.sum(probs * grad_prob, axis=0, keepdims=True)
        dscore = (probs * (grad_prob - delta)).astype(jnp.bfloat16)
        dquery = lax.dot_general(dscore, k, TN, preferred_element_type=jnp.float32) * SCALE
        dkey = jnp.dot(dscore, q, preferred_element_type=jnp.float32) * SCALE
        dvalue = jnp.dot(probs.astype(jnp.bfloat16), g, preferred_element_type=jnp.float32)
        for half in range(2):
            for j in range(GROUP):
                at = slice((h * GROUP + j) * HEAD_DIM, (h * GROUP + j + 1) * HEAD_DIM)
                row = (half * GROUP + j) * BLK
                grad = g[row : row + BLK].astype(jnp.float32)
                total = grad + gain[:, at] * dquery[row : row + BLK]
                total = total.astype(jnp.bfloat16)
                both[half, :, at] = total
                if half == 1:
                    other[:, at] = total
        for d in range(4):
            rows_at = slice(2 * BLK * d, 2 * BLK * (d + 1))
            backs[d][:, k_at] = dkey[rows_at].astype(backs[d].dtype)
            backs[d][:, v_at] = dvalue[rows_at].astype(backs[d].dtype)
        for s in range(4):
            rows_at = slice(8 * BLK + BLK * s, 8 * BLK + BLK * (s + 1))
            parts[s][:, k_at] = dkey[rows_at].astype(parts[s].dtype)
            parts[s][:, v_at] = dvalue[rows_at].astype(parts[s].dtype)


WHOLE = pl.BlockSpec(memory_space=pltpu.VMEM)
FAR = pl.BlockSpec(memory_space=pltpu.HBM)
SCALAR = pl.BlockSpec(memory_space=pltpu.SMEM)
WIDE = 2 * HALF_KV


def shape(dims, dtype):
    return jax.ShapeDtypeStruct(dims, dtype)


def attention(tick, meta, gain, keep, recv, grads, pairs, strided, earlier):
    def at(lead, *rest):
        return pl.BlockSpec((None,) + rest, lambda n: (lead, 0, 0))

    args = [meta, gain, keep, recv]
    specs = [SCALAR, WHOLE, WHOLE, WHOLE]
    if tick:
        args.append(grads)
        specs.append(WHOLE)
    args += list(pairs) + list(strided)
    specs += [at(tick, 2 * BLK, WIDE)] * 4 + [at(tick, BLK, WIDE)] * 4
    bf16, f32 = jnp.bfloat16, jnp.float32
    out_shape = [shape((2, BLK, HALF_FEAT), bf16)]
    if earlier is None:
        out_shape += [shape((BLK, HALF_FEAT), bf16)] + [shape((2 * BLK, WIDE), bf16)] * 3
    else:
        args += earlier
        specs += [WHOLE] * 4
        out_shape += [shape((2, BLK, HALF_FEAT), bf16)] + [shape((2, 2 * BLK, WIDE), bf16)] * 3
    out_shape += [shape((2 * BLK, WIDE), f32), shape((BLK, WIDE), f32)]
    out_shape += [shape((BLK, WIDE), bf16)] * 3
    return pl.pallas_call(
        functools.partial(attention_kernel, tick),
        out_shape=out_shape,
        grid=(1,),
        in_specs=specs,
        out_specs=[WHOLE] * len(out_shape),
        compiler_params=pltpu.CompilerParams(vmem_limit_bytes=32 << 20),
        cost_estimate=pl.CostEstimate(
            flops=2 * 5 * 2 * 512 * 768 * 128, bytes_accessed=4 << 20, transcendentals=2 * 512 * 768
        ),
        name="attention",
    )(*args)


def far_scratch(arrays):
    buffers = [pltpu.VMEM(a.shape, a.dtype) for a in arrays]
    return buffers + [pltpu.SemaphoreType.DMA((len(arrays),))]


def simple(kernel, out_shape, args, scalars=1, far=False):
    size = sum(a.size * a.dtype.itemsize for a in list(args) + list(out_shape))
    return pl.pallas_call(
        kernel,
        out_shape=out_shape,
        in_specs=[SCALAR] * scalars + [FAR if far else WHOLE] * (len(args) - scalars),
        out_specs=[WHOLE] * len(out_shape),
        scratch_shapes=far_scratch(args[scalars:]) if far else [],
        compiler_params=pltpu.CompilerParams(vmem_limit_bytes=16 << 20),
        cost_estimate=pl.CostEstimate(flops=size, bytes_accessed=size, transcendentals=0),
        name=kernel.__name__,
    )(*args)


def column_sum(*refs):
    wide_out, send_out = refs[8:]
    for t in range(2):
        total = refs[4 * t][...]
        for s in range(1, 4):
            total = total + refs[4 * t + s][...].astype(jnp.float32)
        wide_out[t] = total
        send_out[t] = total.astype(jnp.bfloat16)


def split_all(meta, *refs):
    sources, (keep, give, kv_keep, kv_give), buffers, sems = refs[:5], refs[5:9], refs[9:14], refs[14]
    copies = [
        pltpu.make_async_copy(source, buffer, sems.at[n])
        for n, (source, buffer) in enumerate(zip(sources, buffers))
    ]
    for copy in copies:
        copy.start()
    for copy in copies:
        copy.wait()
    keys, values, inputs, first, head = buffers
    swap = meta[0] % 2 == 1
    for source, at in ((keys, 0), (values, HALF_KV)):
        low, high = source[0, :, :, :HALF_KV], source[0, :, :, HALF_KV:]
        mine, far = jnp.where(swap, high, low), jnp.where(swap, low, high)
        keep[:2, :, at : at + HALF_KV] = mine
        give[:2, :, at : at + HALF_KV] = far
        kv_keep[:, :, at : at + HALF_KV] = mine
        kv_give[:, :, at : at + HALF_KV] = far
    for n, source in enumerate((inputs.at[0, 0], inputs.at[0, 1], first.at[0], head.at[0])):
        for h in range(HALF_HEADS):
            low = source[:, h * WIDE : (h + 1) * WIDE]
            high = source[:, HALF_FEAT + h * WIDE : HALF_FEAT + (h + 1) * WIDE]
            keep[2 + 2 * n + h] = jnp.where(swap, high, low)
            give[2 + 2 * n + h] = jnp.where(swap, low, high)


def pair_keys(meta, keep, recv, up_low, up_high, pair, start):
    keep, recv = keep.at[:2], recv.at[:2]
    core = meta[0] % 2
    even = (meta[0] // 8) % 2 == 0
    pair[:, :BLK] = keep[...]
    pair[:, BLK:] = recv[...]
    near = jnp.where(core == 0, keep[...], recv[...])
    above = jnp.where(core == 0, up_low[...], up_high[...])
    start[...] = jnp.where(even, near, above)


def choose(meta, start, x1, x2, x3, out):
    place = (meta[0] // 2) % 4
    near = jnp.where(place == 0, start[...], x1[...])
    far = jnp.where(place == 2, x2[...], x3[...])
    out[...] = jnp.where(place < 2, near, far)


def row_sum(meta, *refs):
    total, x1, x2, x3, own0, own1, back1, back2, back3, far_rows = refs[:10]
    mine_out, swap_out, strided_out = refs[10:]
    index = meta[0]
    owner = (index // 2) % 4 == 0
    even = (index // 8) % 2 == 0
    first = (owner & even & (index % 2 == 0)).astype(jnp.float32)
    second = (owner & even & (index % 2 == 1)).astype(jnp.float32)
    for t, own in enumerate((own0, own1)):
        strided = total[t]
        for x in (x1, x2, x3):
            strided = strided + x[t].astype(jnp.float32)
        strided_out[t] = strided.astype(jnp.bfloat16)
        near = own[...]
        for back in (back1, back2, back3):
            near = near + back[t].astype(jnp.float32)
        mine_out[t] = near[:BLK] + first * strided
        swap_out[t, :, :HALF_FEAT] = far_rows[t]
        swap_out[t, :, HALF_FEAT:] = (near[BLK:] + second * strided).astype(jnp.bfloat16)


def finish(meta, mine, swapped, low, high, mine0, mine1, rows_out, keys_out, values_out):
    swap = meta[0] % 2 == 1
    for t, rows in enumerate((mine0, mine1)):
        other = swapped[t, :, HALF_FEAT:].astype(jnp.float32)
        own = (mine[t] + low[t].astype(jnp.float32)).astype(jnp.bfloat16)
        far = (other + high[t].astype(jnp.float32)).astype(jnp.bfloat16)
        left, right = jnp.where(swap, far, own), jnp.where(swap, own, far)
        for out, at in ((keys_out, 0), (values_out, HALF_KV)):
            out[0, t, :, :HALF_KV] = left[:, at : at + HALF_KV]
            out[0, t, :, HALF_KV:] = right[:, at : at + HALF_KV]
        near, far = rows[0], swapped[t, :, :HALF_FEAT]
        rows_out[0, t, :, :HALF_FEAT] = jnp.where(swap, far, near)
        rows_out[0, t, :, HALF_FEAT:] = jnp.where(swap, near, far)


def body(inputs, saved_keys, saved_values, query_gain, first_grads, head_grads, window, stride):
    index = lax.axis_index("ctx")
    section = lax.axis_index("pp")
    last = lax.axis_size("pp") - 1
    core = index % 2
    place = (index // 2) % 4
    f32, bf16 = jnp.float32, jnp.bfloat16

    def ctx(array, move, when=lambda i: True):
        return route(array, "ctx", lambda i: move(i) if when(i) else None)

    spot = index.astype(jnp.int32).reshape(1)
    half = shape((2, BLK, WIDE), bf16)
    ten = shape((10, BLK, WIDE), bf16)
    keep, give, kv_keep, kv_give = simple(
        split_all,
        [ten, ten, half, half],
        [spot, saved_keys, saved_values, inputs, first_grads, head_grads],
        far=True,
    )
    recv = sibling(give)
    up_low = ctx(kv_keep, lambda i: i + 8, lambda i: i % STRIDE == 0)
    up_high = ctx(kv_give, lambda i: i + 9, lambda i: i % STRIDE == 0)
    pair, start = simple(
        pair_keys,
        [shape((2, 2 * BLK, WIDE), bf16), half],
        [spot, keep, recv, up_low, up_high],
    )
    across = [ctx(start, lambda i: i + 2 * d, lambda i: (i // 2) % 4 == 0) for d in range(1, 4)]
    (chosen,) = simple(choose, [half], [spot, start] + across)
    pairs = [pair] + [ctx(pair, lambda i: i + 2 * d) for d in range(1, 4)]
    strided = [chosen]
    for s in range(1, 4):
        sent = chosen
        if s == 1:
            sent, pairs[TA] = lax.optimization_barrier((chosen, pairs[TA]))
        strided.append(ctx(sent, lambda i: i + STRIDE * s))

    gain = jnp.where(core == 0, query_gain[:, :HALF_FEAT], query_gain[:, HALF_FEAT:])
    heads = jnp.where(core == 0, window[0, :2], window[0, 2:])
    steps = jnp.where(core == 0, stride[0, :2], stride[0, 2:])
    top = jnp.where(section == last, 1, 0)
    meta = jnp.concatenate([jnp.stack([index, top]).astype(jnp.int32), heads, steps])

    first = attention(0, meta, gain, keep, recv, None, pairs, strided, None)
    grads = route(first[0], "pp", lambda i: i - 1)
    columns = [ctx(first[6 + s], lambda i: i - STRIDE * s) for s in range(1, 4)]
    grads, columns = lax.optimization_barrier((grads, columns))
    second = attention(1, meta, gain, keep, recv, grads, pairs, strided, first[1:5])
    columns = [first[6]] + columns + [second[6]]
    columns += [ctx(second[6 + s], lambda i: i - STRIDE * s) for s in range(1, 4)]
    backs = [ctx(second[1 + d], lambda i: i - 2 * d) for d in range(1, 4)]

    wide = shape((2, BLK, WIDE), f32)
    total, send = simple(column_sum, [wide, half], columns, 0)
    rows = []
    for d in range(1, 4):
        rows.append(ctx(send, lambda i: i - 2 * d, lambda i: (i // 2) % 4 == d))
    mine, swap, down = simple(
        row_sum,
        [wide, shape((2, BLK, HALF_FEAT + WIDE), bf16), half],
        [spot, total] + rows + [first[5], second[5]] + backs + [second[1]],
    )
    swapped = sibling(swap)
    low = ctx(down, lambda i: i - 8, lambda i: i % STRIDE == 8)
    high = ctx(down, lambda i: i - 9, lambda i: i % STRIDE == 9)
    keys_shape = shape(saved_keys.shape, bf16)
    grads_out, key_grads, value_grads = simple(
        finish,
        [shape(inputs.shape, bf16), keys_shape, keys_shape],
        [spot, mine, swapped, low, high, first[0], second[0]],
    )
    return grads_out, key_grads, value_grads


def solution(mesh):
    in_specs = (
        P("pp", None, "ctx", None),
        P("pp", None, "ctx", None),
        P("pp", None, "ctx", None),
        P("pp", None),
        P("pp", "ctx", None),
        P(None, "ctx", None),
        P("pp", None),
        P("pp", None),
    )
    out_specs = (P("pp", None, "ctx", None), P("pp", None, "ctx", None), P("pp", None, "ctx", None))
    return jax.shard_map(body, mesh=mesh, in_specs=in_specs, out_specs=out_specs, check_vma=False)
```

```python
import functools

import jax
import jax.numpy as jnp
from jax import lax
from jax.experimental import pallas as pl
from jax.experimental.pallas import tpu as pltpu
from jax.sharding import PartitionSpec as P

BLK = 64
WIN = 7
STRIDE = 16
HEAD_DIM = 128
GROUP = 4
HALF_HEADS = 2
HALF_KV = HALF_HEADS * HEAD_DIM
HALF_FEAT = HALF_HEADS * GROUP * HEAD_DIM
SCALE = HEAD_DIM**-0.5
FARLIM = 56
LOG2E = 1.4426950408889634
NEG = -1e30
NT = (((1,), (1,)), ((), ()))
TN = (((0,), (0,)), ((), ()))


def route(array, axis, move):
    size = lax.axis_size(axis)
    pairs = [(i, move(i)) for i in range(size)]
    return lax.ppermute(array, axis, [(a, b) for a, b in pairs if b is not None and 0 <= b < size])


def sibling(array):
    return route(array, "ctx", lambda i: i ^ 1)


def attention_kernel(tick, meta, gain, keep, recv, *refs):
    if tick:
        grads, refs = refs[0], refs[1:]
    pairs, strided = refs[:4], refs[4:8]
    refs = refs[8:]
    if tick:
        for old, new in zip(refs[:7], refs[8:15]):
            new[0] = old[...]
        refs = refs[7:]
        refs = refs[:1] + tuple(r.at[1] for r in refs[1:8]) + refs[8:]
    both, other, back1, back2, back3, part1, part2, part3, own, part0 = refs
    backs = (own, back1, back2, back3)
    parts = (part0, part1, part2, part3)
    index = meta[0]
    blocks = (index, jnp.bitwise_xor(index, 1))
    group = index // STRIDE
    for h in range(HALF_HEADS):
        window = meta[2 + h]
        stride = meta[4 + h]
        q_rows, g_rows = [], []
        for half, source in enumerate((keep, recv)):
            for j in range(GROUP):
                near = slice(j * HEAD_DIM, (j + 1) * HEAD_DIM)
                at = slice((h * GROUP + j) * HEAD_DIM, (h * GROUP + j + 1) * HEAD_DIM)
                rows = source[2 + 2 * tick + h, :, near].astype(jnp.float32)
                q_rows.append((rows * gain[:, at]).astype(jnp.bfloat16))
                if tick:
                    top = source[8 + h, :, near]
                    g_rows.append(jnp.where(meta[1] == 1, top, grads[half, :, at]))
                else:
                    g_rows.append(source[6 + h, :, near])
        q = jnp.concatenate(q_rows, axis=0)
        g = jnp.concatenate(g_rows, axis=0)
        k_at = slice(h * HEAD_DIM, (h + 1) * HEAD_DIM)
        v_at = slice(HALF_KV + h * HEAD_DIM, HALF_KV + (h + 1) * HEAD_DIM)
        k = jnp.concatenate([r[:, k_at] for r in pairs + strided], axis=0)
        v = jnp.concatenate([r[:, v_at] for r in pairs + strided], axis=0)
        scores = lax.dot_general(k, q, NT, preferred_element_type=jnp.float32)
        wide = GROUP * BLK
        key_row = lax.broadcasted_iota(jnp.int32, (BLK, wide), 0)
        query_row = lax.broadcasted_iota(jnp.int32, (BLK, wide), 1) % BLK
        rows = []
        for slot in range(12):
            cells = []
            for half in range(2):
                query_block = blocks[half]
                if slot < 8:
                    key_block = blocks[slot % 2] - 2 * (slot // 2)
                    gap = query_block - key_block
                    ok = (key_block >= 0) & (gap >= 0) & (gap < WIN)
                    ok = ok & ((gap < window) | (key_block % stride == 0))
                else:
                    key_block = STRIDE * (group - (slot - 8))
                    ok = (key_block >= 0) & (key_block <= query_block - WIN)
                    ok = ok & (key_block % stride == 0)
                cell = scores[slot * BLK : (slot + 1) * BLK, half * wide : (half + 1) * wide]
                if slot == half:
                    cell = jnp.where(key_row <= query_row, cell, NEG)
                else:
                    cell = jnp.where(ok, cell, NEG)
                cells.append(cell)
            rows.append(jnp.concatenate(cells, axis=1))
        scores = jnp.concatenate(rows, axis=0)
        peak = jnp.max(scores, axis=0, keepdims=True)
        weights = jnp.exp2((scores - peak) * (SCALE * LOG2E))
        probs = weights * (1.0 / jnp.sum(weights, axis=0, keepdims=True))
        grad_prob = lax.dot_general(v, g, NT, preferred_element_type=jnp.float32)
        delta = jnp.sum(probs * grad_prob, axis=0, keepdims=True)
        dscore = (probs * (grad_prob - delta)).astype(jnp.bfloat16)
        dquery = lax.dot_general(dscore, k, TN, preferred_element_type=jnp.float32) * SCALE
        dkey = jnp.dot(dscore, q, preferred_element_type=jnp.float32) * SCALE
        dvalue = jnp.dot(probs.astype(jnp.bfloat16), g, preferred_element_type=jnp.float32)
        for half in range(2):
            for j in range(GROUP):
                at = slice((h * GROUP + j) * HEAD_DIM, (h * GROUP + j + 1) * HEAD_DIM)
                row = (half * GROUP + j) * BLK
                grad = g[row : row + BLK].astype(jnp.float32)
                total = grad + gain[:, at] * dquery[row : row + BLK]
                total = total.astype(jnp.bfloat16)
                both[half, :, at] = total
                if half == 1:
                    other[:, at] = total
        for d in range(4):
            rows_at = slice(2 * BLK * d, 2 * BLK * (d + 1))
            backs[d][:, k_at] = dkey[rows_at].astype(backs[d].dtype)
            backs[d][:, v_at] = dvalue[rows_at].astype(backs[d].dtype)
        for s in range(4):
            rows_at = slice(8 * BLK + BLK * s, 8 * BLK + BLK * (s + 1))
            parts[s][:, k_at] = dkey[rows_at].astype(parts[s].dtype)
            parts[s][:, v_at] = dvalue[rows_at].astype(parts[s].dtype)


WHOLE = pl.BlockSpec(memory_space=pltpu.VMEM)
FAR = pl.BlockSpec(memory_space=pltpu.HBM)
SCALAR = pl.BlockSpec(memory_space=pltpu.SMEM)
WIDE = 2 * HALF_KV


def shape(dims, dtype):
    return jax.ShapeDtypeStruct(dims, dtype)


def attention(tick, meta, gain, keep, recv, grads, pairs, strided, earlier):
    def at(lead, *rest):
        return pl.BlockSpec((None,) + rest, lambda n: (lead, 0, 0))

    args = [meta, gain, keep, recv]
    specs = [SCALAR, WHOLE, WHOLE, WHOLE]
    if tick:
        args.append(grads)
        specs.append(WHOLE)
    args += list(pairs) + list(strided)
    specs += [at(tick, 2 * BLK, WIDE)] * 4 + [at(tick, BLK, WIDE)] * 4
    bf16, f32 = jnp.bfloat16, jnp.float32
    out_shape = [shape((2, BLK, HALF_FEAT), bf16)]
    lead = (2,) if tick else ()
    if tick:
        args += earlier
        specs += [WHOLE] * 7
    out_shape.append(shape(lead + (BLK, HALF_FEAT), bf16))
    out_shape += [shape(lead + (2 * BLK, WIDE), bf16)] * 3
    out_shape += [shape(lead + (BLK, WIDE), bf16)] * 3
    out_shape += [shape((2 * BLK, WIDE), f32), shape((BLK, WIDE), f32)]
    return pl.pallas_call(
        functools.partial(attention_kernel, tick),
        out_shape=out_shape,
        grid=(1,),
        in_specs=specs,
        out_specs=[WHOLE] * len(out_shape),
        compiler_params=pltpu.CompilerParams(vmem_limit_bytes=32 << 20),
        cost_estimate=pl.CostEstimate(
            flops=2 * 5 * 2 * 512 * 768 * 128, bytes_accessed=4 << 20, transcendentals=2 * 512 * 768
        ),
        name="attention",
    )(*args)


def far_scratch(arrays):
    buffers = [pltpu.VMEM(a.shape, a.dtype) for a in arrays]
    return buffers + [pltpu.SemaphoreType.DMA((len(arrays),))]


def simple(kernel, out_shape, args, scalars=1, far=False):
    size = sum(a.size * a.dtype.itemsize for a in list(args) + list(out_shape))
    return pl.pallas_call(
        kernel,
        out_shape=out_shape,
        in_specs=[SCALAR] * scalars + [FAR if far else WHOLE] * (len(args) - scalars),
        out_specs=[WHOLE] * len(out_shape),
        scratch_shapes=far_scratch(args[scalars:]) if far else [],
        compiler_params=pltpu.CompilerParams(vmem_limit_bytes=(FARLIM if far else 16) << 20),
        cost_estimate=pl.CostEstimate(flops=size, bytes_accessed=size, transcendentals=0),
        name=kernel.__name__,
    )(*args)


def column_sum(own0, own1, x1, x2, x3, wide_out, send_out):
    for t, own in enumerate((own0, own1)):
        total = own[...]
        for x in (x1, x2, x3):
            total = total + x[t].astype(jnp.float32)
        wide_out[t] = total
        send_out[t] = total.astype(jnp.bfloat16)


def split_all(meta, *refs):
    sources, (keep, give), buffers, sems = refs[:5], refs[5:7], refs[7:12], refs[12]
    copies = [
        pltpu.make_async_copy(source, buffer, sems.at[n])
        for n, (source, buffer) in enumerate(zip(sources, buffers))
    ]
    for copy in copies:
        copy.start()
    for copy in copies:
        copy.wait()
    keys, values, inputs, first, head = buffers
    swap = meta[0] % 2 == 1
    for source, at in ((keys, 0), (values, HALF_KV)):
        low, high = source[0, :, :, :HALF_KV], source[0, :, :, HALF_KV:]
        mine, far = jnp.where(swap, high, low), jnp.where(swap, low, high)
        keep[:2, :, at : at + HALF_KV] = mine
        give[:2, :, at : at + HALF_KV] = far
    for n, source in enumerate((inputs.at[0, 0], inputs.at[0, 1], first.at[0], head.at[0])):
        for h in range(HALF_HEADS):
            low = source[:, h * WIDE : (h + 1) * WIDE]
            high = source[:, HALF_FEAT + h * WIDE : HALF_FEAT + (h + 1) * WIDE]
            keep[2 + 2 * n + h] = jnp.where(swap, high, low)
            give[2 + 2 * n + h] = jnp.where(swap, low, high)


def pair_keys(meta, keep, recv, pair):
    pair[:, :BLK] = keep[:2]
    pair[:, BLK:] = recv[:2]


def choose(meta, p0, p1, p2, p3, out):
    core = meta[0] % 2
    place = (meta[0] // 2) % 4
    for n, pair in enumerate((p0, p1, p2, p3)):
        @pl.when(place == n)
        def _():
            out[...] = jnp.where(core == 0, pair[:, :BLK], pair[:, BLK:])


def add_strided(meta, total, below, back1, back2, back3, own0, own1, out1, out2, out3, near):
    core = meta[0] % 2
    place = (meta[0] // 2) % 4
    even = (meta[0] // 8) % 2 == 0
    for t, own in enumerate((own0, own1)):
        strided = total[t] + below[t].astype(jnp.float32)
        halves = [jnp.where(even & (core == k), strided, 0.0) for k in range(2)]
        spread = jnp.concatenate(halves, axis=0)
        near[t] = own[...] + jnp.where(place == 0, spread, 0.0)
        for d, (back, out) in enumerate(((back1, out1), (back2, out2), (back3, out3))):
            held = back[t].astype(jnp.float32) + jnp.where(place == d + 1, spread, 0.0)
            out[t] = held.astype(jnp.bfloat16)


def row_sum(meta, near, back1, back2, back3, far_rows, mine_out, swap_out):
    for t in range(2):
        total = near[t]
        for back in (back1, back2, back3):
            total = total + back[t].astype(jnp.float32)
        mine_out[t] = total[:BLK]
        swap_out[t, :, :HALF_FEAT] = far_rows[t]
        swap_out[t, :, HALF_FEAT:] = total[BLK:].astype(jnp.bfloat16)


def finish(meta, mine, swapped, mine0, mine1, rows_out, keys_out, values_out):
    swap = meta[0] % 2 == 1
    for t, rows in enumerate((mine0, mine1)):
        own = mine[t].astype(jnp.bfloat16)
        far = swapped[t, :, HALF_FEAT:]
        left, right = jnp.where(swap, far, own), jnp.where(swap, own, far)
        for out, at in ((keys_out, 0), (values_out, HALF_KV)):
            out[0, t, :, :HALF_KV] = left[:, at : at + HALF_KV]
            out[0, t, :, HALF_KV:] = right[:, at : at + HALF_KV]
        near, far = rows[0], swapped[t, :, :HALF_FEAT]
        rows_out[0, t, :, :HALF_FEAT] = jnp.where(swap, far, near)
        rows_out[0, t, :, HALF_FEAT:] = jnp.where(swap, near, far)


def body(inputs, saved_keys, saved_values, query_gain, first_grads, head_grads, window, stride):
    index = lax.axis_index("ctx")
    section = lax.axis_index("pp")
    last = lax.axis_size("pp") - 1
    core = index % 2
    place = (index // 2) % 4
    f32, bf16 = jnp.float32, jnp.bfloat16

    def ctx(array, move, when=lambda i: True):
        return route(array, "ctx", lambda i: move(i) if when(i) else None)

    spot = index.astype(jnp.int32).reshape(1)
    half = shape((2, BLK, WIDE), bf16)
    ten = shape((10, BLK, WIDE), bf16)
    keep, give = simple(
        split_all,
        [ten, ten],
        [spot, saved_keys, saved_values, inputs, first_grads, head_grads],
        far=True,
    )
    recv = sibling(give)
    (pair,) = simple(pair_keys, [shape((2, 2 * BLK, WIDE), bf16)], [spot, keep, recv])
    pairs = [pair] + [ctx(pair, lambda i: i + 2 * d) for d in range(1, 4)]
    (chosen,) = simple(choose, [half], [spot] + pairs)
    above = ctx(chosen, lambda i: i + 8, lambda i: (i // 8) % 2 == 0)
    chosen = jnp.where((index // 8) % 2 == 0, chosen, above)
    strided = [chosen] + [ctx(chosen, lambda i: i + STRIDE * s) for s in range(1, 4)]
    gain = jnp.where(core == 0, query_gain[:, :HALF_FEAT], query_gain[:, HALF_FEAT:])
    heads = jnp.where(core == 0, window[0, :2], window[0, 2:])
    steps = jnp.where(core == 0, stride[0, :2], stride[0, 2:])
    top = jnp.where(section == last, 1, 0)
    meta = jnp.concatenate([jnp.stack([index, top]).astype(jnp.int32), heads, steps])

    first = attention(0, meta, gain, keep, recv, None, pairs, strided, None)
    grads = route(first[0], "pp", lambda i: i - 1)
    second = attention(1, meta, gain, keep, recv, grads, pairs, strided, first[1:8])
    columns = [first[9], second[9]]
    columns += [ctx(second[4 + s], lambda i: i - STRIDE * s) for s in range(1, 4)]
    wide = shape((2, BLK, WIDE), f32)
    total, send = simple(column_sum, [wide, half], columns, 0)
    below = ctx(send, lambda i: i - 8, lambda i: (i // 8) % 2 == 1)
    full = shape((2, 2 * BLK, WIDE), bf16)
    *backs, near = simple(
        add_strided,
        [full, full, full, shape((2, 2 * BLK, WIDE), f32)],
        [spot, total, below] + list(second[2:5]) + [first[8], second[8]],
    )
    backs = [ctx(backs[d - 1], lambda i: i - 2 * d) for d in range(1, 4)]
    mine, swap = simple(
        row_sum,
        [wide, shape((2, BLK, HALF_FEAT + WIDE), bf16)],
        [spot, near] + backs + [second[1]],
    )
    swapped = sibling(swap)
    keys_shape = shape(saved_keys.shape, bf16)
    grads_out, key_grads, value_grads = simple(
        finish,
        [shape(inputs.shape, bf16), keys_shape, keys_shape],
        [spot, mine, swapped, first[0], second[0]],
    )
    return grads_out, key_grads, value_grads


def solution(mesh):
    in_specs = (
        P("pp", None, "ctx", None),
        P("pp", None, "ctx", None),
        P("pp", None, "ctx", None),
        P("pp", None),
        P("pp", "ctx", None),
        P(None, "ctx", None),
        P("pp", None),
        P("pp", None),
    )
    out_specs = (P("pp", None, "ctx", None), P("pp", None, "ctx", None), P("pp", None, "ctx", None))
    return jax.shard_map(body, mesh=mesh, in_specs=in_specs, out_specs=out_specs, check_vma=False)
```

```python
import functools

import jax
import jax.numpy as jnp
from jax import lax
from jax.experimental import pallas as pl
from jax.experimental.pallas import tpu as pltpu
from jax.sharding import PartitionSpec as P

BLK = 64
WIN = 7
STRIDE = 16
HEAD_DIM = 128
GROUP = 4
HALF_HEADS = 2
HALF_KV = HALF_HEADS * HEAD_DIM
HALF_FEAT = HALF_HEADS * GROUP * HEAD_DIM
SCALE = HEAD_DIM**-0.5
FARLIM = 56
LOG2E = 1.4426950408889634
NEG = -1e30
NT = (((1,), (1,)), ((), ()))
TN = (((0,), (0,)), ((), ()))


def route(array, axis, move):
    size = lax.axis_size(axis)
    pairs = [(i, move(i)) for i in range(size)]
    return lax.ppermute(array, axis, [(a, b) for a, b in pairs if b is not None and 0 <= b < size])


def sibling(array):
    return route(array, "ctx", lambda i: i ^ 1)


def attention_kernel(tick, meta, gain, keep, recv, *refs):
    if tick:
        grads, refs = refs[0], refs[1:]
    pairs, shifts = refs[:4], refs[4:12]
    refs = refs[12:]
    if tick:
        for old, new in zip(refs[:8], refs[9:17]):
            new[0] = old[...]
        refs = refs[8:]
        refs = refs[:1] + tuple(r.at[1] for r in refs[1:9]) + refs[9:]
    both, other, back1, back2, back3, part0, part1, part2, part3, own = refs
    backs = (own, back1, back2, back3)
    parts = (part0, part1, part2, part3)
    index = meta[0]
    blocks = (index, jnp.bitwise_xor(index, 1))
    group = index // STRIDE
    even = (index // 8) % 2 == 0
    strided = [jnp.where(even, shifts[2 * n][...], shifts[2 * n + 1][...]) for n in range(4)]
    for h in range(HALF_HEADS):
        window = meta[2 + h]
        stride = meta[4 + h]
        q_rows, g_rows = [], []
        for half, source in enumerate((keep, recv)):
            for j in range(GROUP):
                near = slice(j * HEAD_DIM, (j + 1) * HEAD_DIM)
                at = slice((h * GROUP + j) * HEAD_DIM, (h * GROUP + j + 1) * HEAD_DIM)
                rows = source[2 + 2 * tick + h, :, near].astype(jnp.float32)
                q_rows.append((rows * gain[:, at]).astype(jnp.bfloat16))
                if tick:
                    top = source[8 + h, :, near]
                    g_rows.append(jnp.where(meta[1] == 1, top, grads[half, :, at]))
                else:
                    g_rows.append(source[6 + h, :, near])
        q = jnp.concatenate(q_rows, axis=0)
        g = jnp.concatenate(g_rows, axis=0)
        k_at = slice(h * HEAD_DIM, (h + 1) * HEAD_DIM)
        v_at = slice(HALF_KV + h * HEAD_DIM, HALF_KV + (h + 1) * HEAD_DIM)
        k = jnp.concatenate([r[:, k_at] for r in list(pairs) + strided], axis=0)
        v = jnp.concatenate([r[:, v_at] for r in list(pairs) + strided], axis=0)
        scores = lax.dot_general(k, q, NT, preferred_element_type=jnp.float32)
        wide = GROUP * BLK
        key_row = lax.broadcasted_iota(jnp.int32, (BLK, wide), 0)
        query_row = lax.broadcasted_iota(jnp.int32, (BLK, wide), 1) % BLK
        rows = []
        for slot in range(12):
            cells = []
            for half in range(2):
                query_block = blocks[half]
                if slot < 8:
                    key_block = blocks[slot % 2] - 2 * (slot // 2)
                    gap = query_block - key_block
                    ok = (key_block >= 0) & (gap >= 0) & (gap < WIN)
                    ok = ok & ((gap < window) | (key_block % stride == 0))
                else:
                    key_block = STRIDE * (group - (slot - 8))
                    ok = (key_block >= 0) & (key_block <= query_block - WIN)
                    ok = ok & (key_block % stride == 0)
                cell = scores[slot * BLK : (slot + 1) * BLK, half * wide : (half + 1) * wide]
                if slot == half:
                    cell = jnp.where(key_row <= query_row, cell, NEG)
                else:
                    cell = jnp.where(ok, cell, NEG)
                cells.append(cell)
            rows.append(jnp.concatenate(cells, axis=1))
        scores = jnp.concatenate(rows, axis=0)
        peak = jnp.max(scores, axis=0, keepdims=True)
        weights = jnp.exp2((scores - peak) * (SCALE * LOG2E))
        probs = weights * (1.0 / jnp.sum(weights, axis=0, keepdims=True))
        grad_prob = lax.dot_general(v, g, NT, preferred_element_type=jnp.float32)
        delta = jnp.sum(probs * grad_prob, axis=0, keepdims=True)
        dscore = (probs * (grad_prob - delta)).astype(jnp.bfloat16)
        dquery = lax.dot_general(dscore, k, TN, preferred_element_type=jnp.float32) * SCALE
        dkey = jnp.dot(dscore, q, preferred_element_type=jnp.float32) * SCALE
        dvalue = jnp.dot(probs.astype(jnp.bfloat16), g, preferred_element_type=jnp.float32)
        for half in range(2):
            for j in range(GROUP):
                at = slice((h * GROUP + j) * HEAD_DIM, (h * GROUP + j + 1) * HEAD_DIM)
                row = (half * GROUP + j) * BLK
                grad = g[row : row + BLK].astype(jnp.float32)
                total = grad + gain[:, at] * dquery[row : row + BLK]
                total = total.astype(jnp.bfloat16)
                both[half, :, at] = total
                if half == 1:
                    other[:, at] = total
        for d in range(4):
            rows_at = slice(2 * BLK * d, 2 * BLK * (d + 1))
            backs[d][:, k_at] = dkey[rows_at].astype(backs[d].dtype)
            backs[d][:, v_at] = dvalue[rows_at].astype(backs[d].dtype)
        for s in range(4):
            rows_at = slice(8 * BLK + BLK * s, 8 * BLK + BLK * (s + 1))
            parts[s][:, k_at] = dkey[rows_at].astype(parts[s].dtype)
            parts[s][:, v_at] = dvalue[rows_at].astype(parts[s].dtype)


WHOLE = pl.BlockSpec(memory_space=pltpu.VMEM)
FAR = pl.BlockSpec(memory_space=pltpu.HBM)
SCALAR = pl.BlockSpec(memory_space=pltpu.SMEM)
WIDE = 2 * HALF_KV


def shape(dims, dtype):
    return jax.ShapeDtypeStruct(dims, dtype)


def attention(tick, meta, gain, keep, recv, grads, pairs, strided, earlier):
    def at(lead, *rest):
        return pl.BlockSpec((None,) + rest, lambda n: (lead, 0, 0))

    args = [meta, gain, keep, recv]
    specs = [SCALAR, WHOLE, WHOLE, WHOLE]
    if tick:
        args.append(grads)
        specs.append(WHOLE)
    args += list(pairs) + list(strided)
    specs += [at(tick, 2 * BLK, WIDE)] * 4 + [at(tick, BLK, WIDE)] * 8
    bf16, f32 = jnp.bfloat16, jnp.float32
    out_shape = [shape((2, BLK, HALF_FEAT), bf16)]
    lead = (2,) if tick else ()
    if tick:
        args += earlier
        specs += [WHOLE] * 8
    out_shape.append(shape(lead + (BLK, HALF_FEAT), bf16))
    out_shape += [shape(lead + (2 * BLK, WIDE), bf16)] * 3
    out_shape += [shape(lead + (BLK, WIDE), bf16)] * 4
    out_shape.append(shape((2 * BLK, WIDE), f32))
    return pl.pallas_call(
        functools.partial(attention_kernel, tick),
        out_shape=out_shape,
        grid=(1,),
        in_specs=specs,
        out_specs=[WHOLE] * len(out_shape),
        compiler_params=pltpu.CompilerParams(vmem_limit_bytes=32 << 20),
        cost_estimate=pl.CostEstimate(
            flops=2 * 5 * 2 * 512 * 768 * 128, bytes_accessed=4 << 20, transcendentals=2 * 512 * 768
        ),
        name="attention",
    )(*args)


def far_scratch(arrays):
    buffers = [pltpu.VMEM(a.shape, a.dtype) for a in arrays]
    return buffers + [pltpu.SemaphoreType.DMA((len(arrays),))]


def simple(kernel, out_shape, args, scalars=1, far=False):
    size = sum(a.size * a.dtype.itemsize for a in list(args) + list(out_shape))
    return pl.pallas_call(
        kernel,
        out_shape=out_shape,
        in_specs=[SCALAR] * scalars + [FAR if far else WHOLE] * (len(args) - scalars),
        out_specs=[WHOLE] * len(out_shape),
        scratch_shapes=far_scratch(args[scalars:]) if far else [],
        compiler_params=pltpu.CompilerParams(vmem_limit_bytes=(FARLIM if far else 16) << 20),
        cost_estimate=pl.CostEstimate(flops=size, bytes_accessed=size, transcendentals=0),
        name=kernel.__name__,
    )(*args)


def split_all(meta, *refs):
    sources, (keep, give), buffers, sems = refs[:5], refs[5:7], refs[7:12], refs[12]
    copies = [
        pltpu.make_async_copy(source, buffer, sems.at[n])
        for n, (source, buffer) in enumerate(zip(sources, buffers))
    ]
    for copy in copies:
        copy.start()
    for copy in copies:
        copy.wait()
    keys, values, inputs, first, head = buffers
    swap = meta[0] % 2 == 1
    for source, at in ((keys, 0), (values, HALF_KV)):
        low, high = source[0, :, :, :HALF_KV], source[0, :, :, HALF_KV:]
        mine, far = jnp.where(swap, high, low), jnp.where(swap, low, high)
        keep[:2, :, at : at + HALF_KV] = mine
        give[:2, :, at : at + HALF_KV] = far
    for n, source in enumerate((inputs.at[0, 0], inputs.at[0, 1], first.at[0], head.at[0])):
        for h in range(HALF_HEADS):
            low = source[:, h * WIDE : (h + 1) * WIDE]
            high = source[:, HALF_FEAT + h * WIDE : HALF_FEAT + (h + 1) * WIDE]
            keep[2 + 2 * n + h] = jnp.where(swap, high, low)
            give[2 + 2 * n + h] = jnp.where(swap, low, high)


def pair_keys(meta, keep, recv, pair):
    pair[:, :BLK] = keep[:2]
    pair[:, BLK:] = recv[:2]


def choose(meta, p0, p1, p2, p3, out):
    core = meta[0] % 2
    place = (meta[0] // 2) % 4
    for n, pair in enumerate((p0, p1, p2, p3)):
        @pl.when(place == n)
        def _():
            out[...] = jnp.where(core == 0, pair[:, :BLK], pair[:, BLK:])


def add_strided(meta, *refs):
    parts, (back1, back2, back3, own0, own1), (out1, out2, out3, near) = refs[:8], refs[8:13], refs[13:]
    core = meta[0] % 2
    place = (meta[0] // 2) % 4
    even = (meta[0] // 8) % 2 == 0
    for t, own in enumerate((own0, own1)):
        strided = parts[0][t].astype(jnp.float32)
        for part in parts[1:]:
            strided = strided + part[t].astype(jnp.float32)
        halves = [jnp.where(even & (core == k), strided, 0.0) for k in range(2)]
        spread = jnp.concatenate(halves, axis=0)
        near[t] = own[...] + jnp.where(place == 0, spread, 0.0)
        for d, (back, out) in enumerate(((back1, out1), (back2, out2), (back3, out3))):
            held = back[t].astype(jnp.float32) + jnp.where(place == d + 1, spread, 0.0)
            out[t] = held.astype(jnp.bfloat16)


def row_sum(meta, near, back1, back2, back3, far_rows, mine_out, swap_out):
    for t in range(2):
        total = near[t]
        for back in (back1, back2, back3):
            total = total + back[t].astype(jnp.float32)
        mine_out[t] = total[:BLK]
        swap_out[t, :, :HALF_FEAT] = far_rows[t]
        swap_out[t, :, HALF_FEAT:] = total[BLK:].astype(jnp.bfloat16)


def finish(meta, mine, swapped, mine0, mine1, rows_out, keys_out, values_out):
    swap = meta[0] % 2 == 1
    for t, rows in enumerate((mine0, mine1)):
        own = mine[t].astype(jnp.bfloat16)
        far = swapped[t, :, HALF_FEAT:]
        left, right = jnp.where(swap, far, own), jnp.where(swap, own, far)
        for out, at in ((keys_out, 0), (values_out, HALF_KV)):
            out[0, t, :, :HALF_KV] = left[:, at : at + HALF_KV]
            out[0, t, :, HALF_KV:] = right[:, at : at + HALF_KV]
        near, far = rows[0], swapped[t, :, :HALF_FEAT]
        rows_out[0, t, :, :HALF_FEAT] = jnp.where(swap, far, near)
        rows_out[0, t, :, HALF_FEAT:] = jnp.where(swap, near, far)


def body(inputs, saved_keys, saved_values, query_gain, first_grads, head_grads, window, stride):
    index = lax.axis_index("ctx")
    section = lax.axis_index("pp")
    last = lax.axis_size("pp") - 1
    core = index % 2
    place = (index // 2) % 4
    f32, bf16 = jnp.float32, jnp.bfloat16

    def ctx(array, move, when=lambda i: True):
        return route(array, "ctx", lambda i: move(i) if when(i) else None)

    spot = index.astype(jnp.int32).reshape(1)
    half = shape((2, BLK, WIDE), bf16)
    ten = shape((10, BLK, WIDE), bf16)
    keep, give = simple(
        split_all,
        [ten, ten],
        [spot, saved_keys, saved_values, inputs, first_grads, head_grads],
        far=True,
    )
    recv = sibling(give)
    (pair,) = simple(pair_keys, [shape((2, 2 * BLK, WIDE), bf16)], [spot, keep, recv])
    pairs = [pair] + [ctx(pair, lambda i: i + 2 * d) for d in range(1, 4)]
    (chosen,) = simple(choose, [half], [spot] + pairs)
    def on_even(i):
        return (i // 8) % 2 == 0

    strided = [chosen] + [ctx(chosen, lambda i: i + 8 * s, on_even) for s in range(1, 8)]
    gain = jnp.where(core == 0, query_gain[:, :HALF_FEAT], query_gain[:, HALF_FEAT:])
    heads = jnp.where(core == 0, window[0, :2], window[0, 2:])
    steps = jnp.where(core == 0, stride[0, :2], stride[0, 2:])
    top = jnp.where(section == last, 1, 0)
    meta = jnp.concatenate([jnp.stack([index, top]).astype(jnp.int32), heads, steps])

    first = attention(0, meta, gain, keep, recv, None, pairs, strided, None)
    grads = route(first[0], "pp", lambda i: i - 1)
    second = attention(1, meta, gain, keep, recv, grads, pairs, strided, first[1:9])
    parts = [second[5]]
    for s in range(1, 8):
        parts.append(ctx(second[5 + s // 2], lambda i: i - 8 * s, lambda i: on_even(i - 8 * s)))
    wide = shape((2, BLK, WIDE), f32)
    full = shape((2, 2 * BLK, WIDE), bf16)
    *backs, near = simple(
        add_strided,
        [full, full, full, shape((2, 2 * BLK, WIDE), f32)],
        [spot] + parts + list(second[2:5]) + [first[9], second[9]],
    )
    backs = [ctx(backs[d - 1], lambda i: i - 2 * d) for d in range(1, 4)]
    mine, swap = simple(
        row_sum,
        [wide, shape((2, BLK, HALF_FEAT + WIDE), bf16)],
        [spot, near] + backs + [second[1]],
    )
    swapped = sibling(swap)
    keys_shape = shape(saved_keys.shape, bf16)
    grads_out, key_grads, value_grads = simple(
        finish,
        [shape(inputs.shape, bf16), keys_shape, keys_shape],
        [spot, mine, swapped, first[0], second[0]],
    )
    return grads_out, key_grads, value_grads


def solution(mesh):
    in_specs = (
        P("pp", None, "ctx", None),
        P("pp", None, "ctx", None),
        P("pp", None, "ctx", None),
        P("pp", None),
        P("pp", "ctx", None),
        P(None, "ctx", None),
        P("pp", None),
        P("pp", None),
    )
    out_specs = (P("pp", None, "ctx", None), P("pp", None, "ctx", None), P("pp", None, "ctx", None))
    return jax.shard_map(body, mesh=mesh, in_specs=in_specs, out_specs=out_specs, check_vma=False)
```

```python
import functools

import jax
import jax.numpy as jnp
from jax import lax
from jax.experimental import pallas as pl
from jax.experimental.pallas import tpu as pltpu
from jax.sharding import PartitionSpec as P

BLK = 64
WIN = 7
STRIDE = 16
HEAD_DIM = 128
GROUP = 4
HALF_HEADS = 2
HALF_KV = HALF_HEADS * HEAD_DIM
HALF_FEAT = HALF_HEADS * GROUP * HEAD_DIM
SCALE = HEAD_DIM**-0.5
LOG2E = 1.4426950408889634
NEG = -1e30
NT = (((1,), (1,)), ((), ()))
TN = (((0,), (0,)), ((), ()))


def route(array, axis, move):
    size = lax.axis_size(axis)
    pairs = [(i, move(i)) for i in range(size)]
    return lax.ppermute(array, axis, [(a, b) for a, b in pairs if b is not None and 0 <= b < size])


def sibling(array):
    return route(array, "ctx", lambda i: i ^ 1)


def attention_kernel(tick, meta, gain, keep, recv, *refs):
    if tick:
        grads, refs = refs[0], refs[1:]
    pairs, strided = refs[:4], refs[4:8]
    refs = refs[8:]
    if tick:
        for old, new in zip(refs[:7], refs[8:15]):
            new[0] = old[...]
        refs = refs[7:]
        refs = refs[:1] + tuple(r.at[1] for r in refs[1:8]) + refs[8:]
    both, other, back1, back2, back3, part1, part2, part3, own, part0 = refs
    backs = (own, back1, back2, back3)
    parts = (part0, part1, part2, part3)
    index = meta[0]
    blocks = (index, jnp.bitwise_xor(index, 1))
    group = index // STRIDE
    for h in range(HALF_HEADS):
        window = meta[2 + h]
        stride = meta[4 + h]
        q_rows, g_rows = [], []
        for half, source in enumerate((keep, recv)):
            for j in range(GROUP):
                near = slice(j * HEAD_DIM, (j + 1) * HEAD_DIM)
                at = slice((h * GROUP + j) * HEAD_DIM, (h * GROUP + j + 1) * HEAD_DIM)
                rows = source[2 + 2 * tick + h, :, near].astype(jnp.float32)
                q_rows.append((rows * gain[:, at]).astype(jnp.bfloat16))
                if tick:
                    top = source[8 + h, :, near]
                    g_rows.append(jnp.where(meta[1] == 1, top, grads[half, :, at]))
                else:
                    g_rows.append(source[6 + h, :, near])
        q = jnp.concatenate(q_rows, axis=0)
        g = jnp.concatenate(g_rows, axis=0)
        k_at = slice(h * HEAD_DIM, (h + 1) * HEAD_DIM)
        v_at = slice(HALF_KV + h * HEAD_DIM, HALF_KV + (h + 1) * HEAD_DIM)
        k = jnp.concatenate([r[:, k_at] for r in pairs + strided], axis=0)
        v = jnp.concatenate([r[:, v_at] for r in pairs + strided], axis=0)
        scores = lax.dot_general(k, q, NT, preferred_element_type=jnp.float32)
        wide = GROUP * BLK
        key_row = lax.broadcasted_iota(jnp.int32, (BLK, wide), 0)
        query_row = lax.broadcasted_iota(jnp.int32, (BLK, wide), 1) % BLK
        rows = []
        for slot in range(12):
            cells = []
            for half in range(2):
                query_block = blocks[half]
                if slot < 8:
                    key_block = blocks[slot % 2] - 2 * (slot // 2)
                    gap = query_block - key_block
                    ok = (key_block >= 0) & (gap >= 0) & (gap < WIN)
                    ok = ok & ((gap < window) | (key_block % stride == 0))
                else:
                    key_block = STRIDE * (group - (slot - 8))
                    ok = (key_block >= 0) & (key_block <= query_block - WIN)
                    ok = ok & (key_block % stride == 0)
                cell = scores[slot * BLK : (slot + 1) * BLK, half * wide : (half + 1) * wide]
                if slot == half:
                    cell = jnp.where(key_row <= query_row, cell, NEG)
                else:
                    cell = jnp.where(ok, cell, NEG)
                cells.append(cell)
            rows.append(jnp.concatenate(cells, axis=1))
        scores = jnp.concatenate(rows, axis=0)
        peak = jnp.max(scores, axis=0, keepdims=True)
        weights = jnp.exp2((scores - peak) * (SCALE * LOG2E))
        probs = weights * (1.0 / jnp.sum(weights, axis=0, keepdims=True))
        grad_prob = lax.dot_general(v, g, NT, preferred_element_type=jnp.float32)
        delta = jnp.sum(probs * grad_prob, axis=0, keepdims=True)
        dscore = (probs * (grad_prob - delta)).astype(jnp.bfloat16)
        dquery = lax.dot_general(dscore, k, TN, preferred_element_type=jnp.float32) * SCALE
        dkey = jnp.dot(dscore, q, preferred_element_type=jnp.float32) * SCALE
        dvalue = jnp.dot(probs.astype(jnp.bfloat16), g, preferred_element_type=jnp.float32)
        for half in range(2):
            for j in range(GROUP):
                at = slice((h * GROUP + j) * HEAD_DIM, (h * GROUP + j + 1) * HEAD_DIM)
                row = (half * GROUP + j) * BLK
                grad = g[row : row + BLK].astype(jnp.float32)
                total = grad + gain[:, at] * dquery[row : row + BLK]
                total = total.astype(jnp.bfloat16)
                both[half, :, at] = total
                if half == 1:
                    other[:, at] = total
        for d in range(4):
            rows_at = slice(2 * BLK * d, 2 * BLK * (d + 1))
            backs[d][:, k_at] = dkey[rows_at].astype(backs[d].dtype)
            backs[d][:, v_at] = dvalue[rows_at].astype(backs[d].dtype)
        for s in range(4):
            rows_at = slice(8 * BLK + BLK * s, 8 * BLK + BLK * (s + 1))
            parts[s][:, k_at] = dkey[rows_at].astype(parts[s].dtype)
            parts[s][:, v_at] = dvalue[rows_at].astype(parts[s].dtype)


WHOLE = pl.BlockSpec(memory_space=pltpu.VMEM)
FAR = pl.BlockSpec(memory_space=pltpu.HBM)
SCALAR = pl.BlockSpec(memory_space=pltpu.SMEM)
WIDE = 2 * HALF_KV


def shape(dims, dtype):
    return jax.ShapeDtypeStruct(dims, dtype)


def attention(tick, meta, gain, keep, recv, grads, pairs, strided, earlier):
    def at(lead, *rest):
        return pl.BlockSpec((None,) + rest, lambda n: (lead, 0, 0))

    args = [meta, gain, keep, recv]
    specs = [SCALAR, WHOLE, WHOLE, WHOLE]
    if tick:
        args.append(grads)
        specs.append(WHOLE)
    args += list(pairs) + list(strided)
    specs += [at(tick, 2 * BLK, WIDE)] * 4 + [at(tick, BLK, WIDE)] * 4
    bf16, f32 = jnp.bfloat16, jnp.float32
    out_shape = [shape((2, BLK, HALF_FEAT), bf16)]
    lead = (2,) if tick else ()
    if tick:
        args += earlier
        specs += [WHOLE] * 7
    out_shape.append(shape(lead + (BLK, HALF_FEAT), bf16))
    out_shape += [shape(lead + (2 * BLK, WIDE), bf16)] * 3
    out_shape += [shape(lead + (BLK, WIDE), bf16)] * 3
    out_shape += [shape((2 * BLK, WIDE), f32), shape((BLK, WIDE), f32)]
    return pl.pallas_call(
        functools.partial(attention_kernel, tick),
        out_shape=out_shape,
        grid=(1,),
        in_specs=specs,
        out_specs=[WHOLE] * len(out_shape),
        compiler_params=pltpu.CompilerParams(vmem_limit_bytes=32 << 20),
        cost_estimate=pl.CostEstimate(
            flops=2 * 5 * 2 * 512 * 768 * 128, bytes_accessed=4 << 20, transcendentals=2 * 512 * 768
        ),
        name="attention",
    )(*args)


def far_scratch(arrays):
    buffers = [pltpu.VMEM(a.shape, a.dtype) for a in arrays]
    return buffers + [pltpu.SemaphoreType.DMA((len(arrays),))]


def simple(kernel, out_shape, args, scalars=1, far=False):
    size = sum(a.size * a.dtype.itemsize for a in list(args) + list(out_shape))
    return pl.pallas_call(
        kernel,
        out_shape=out_shape,
        in_specs=[SCALAR] * scalars + [FAR if far else WHOLE] * (len(args) - scalars),
        out_specs=[WHOLE] * len(out_shape),
        scratch_shapes=far_scratch(args[scalars:]) if far else [],
        compiler_params=pltpu.CompilerParams(vmem_limit_bytes=(56 if far else 16) << 20),
        cost_estimate=pl.CostEstimate(flops=size, bytes_accessed=size, transcendentals=0),
        name=kernel.__name__,
    )(*args)


def column_sum(own0, own1, x1, x2, x3, wide_out, send_out):
    for t, own in enumerate((own0, own1)):
        total = own[...]
        for x in (x1, x2, x3):
            total = total + x[t].astype(jnp.float32)
        wide_out[t] = total
        send_out[t] = total.astype(jnp.bfloat16)


def split_all(meta, *refs):
    sources, (keep, give, kv_keep, kv_give), buffers, sems = refs[:5], refs[5:9], refs[9:14], refs[14]
    copies = [
        pltpu.make_async_copy(source, buffer, sems.at[n])
        for n, (source, buffer) in enumerate(zip(sources, buffers))
    ]
    for copy in copies:
        copy.start()
    for copy in copies:
        copy.wait()
    keys, values, inputs, first, head = buffers
    swap = meta[0] % 2 == 1
    for source, at in ((keys, 0), (values, HALF_KV)):
        low, high = source[0, :, :, :HALF_KV], source[0, :, :, HALF_KV:]
        mine, far = jnp.where(swap, high, low), jnp.where(swap, low, high)
        keep[:2, :, at : at + HALF_KV] = mine
        give[:2, :, at : at + HALF_KV] = far
        kv_keep[:, :, at : at + HALF_KV] = mine
        kv_give[:, :, at : at + HALF_KV] = far
    for n, source in enumerate((inputs.at[0, 0], inputs.at[0, 1], first.at[0], head.at[0])):
        for h in range(HALF_HEADS):
            low = source[:, h * WIDE : (h + 1) * WIDE]
            high = source[:, HALF_FEAT + h * WIDE : HALF_FEAT + (h + 1) * WIDE]
            keep[2 + 2 * n + h] = jnp.where(swap, high, low)
            give[2 + 2 * n + h] = jnp.where(swap, low, high)


def pair_keys(meta, keep, recv, pair):
    pair[:, :BLK] = keep[:2]
    pair[:, BLK:] = recv[:2]


def first_block(meta, keep, recv, up_low, up_high, start):
    core = meta[0] % 2
    even = (meta[0] // 8) % 2 == 0
    near = jnp.where(core == 0, keep[:2], recv[:2])
    above = jnp.where(core == 0, up_low[...], up_high[...])
    start[...] = jnp.where(even, near, above)


def choose(meta, start, x1, x2, x3, out):
    place = (meta[0] // 2) % 4
    near = jnp.where(place == 0, start[...], x1[...])
    far = jnp.where(place == 2, x2[...], x3[...])
    out[...] = jnp.where(place < 2, near, far)


def row_sum(meta, *refs):
    total, x1, x2, x3, own0, own1, back1, back2, back3, far_rows = refs[:10]
    mine_out, swap_out, strided_out = refs[10:]
    index = meta[0]
    owner = (index // 2) % 4 == 0
    even = (index // 8) % 2 == 0
    first = (owner & even & (index % 2 == 0)).astype(jnp.float32)
    second = (owner & even & (index % 2 == 1)).astype(jnp.float32)
    for t, own in enumerate((own0, own1)):
        strided = total[t]
        for x in (x1, x2, x3):
            strided = strided + x[t].astype(jnp.float32)
        strided_out[t] = strided.astype(jnp.bfloat16)
        near = own[...]
        for back in (back1, back2, back3):
            near = near + back[t].astype(jnp.float32)
        mine_out[t] = near[:BLK] + first * strided
        swap_out[t, :, :HALF_FEAT] = far_rows[t]
        swap_out[t, :, HALF_FEAT:] = (near[BLK:] + second * strided).astype(jnp.bfloat16)


def finish(meta, mine, swapped, low, high, mine0, mine1, rows_out, keys_out, values_out):
    swap = meta[0] % 2 == 1
    for t, rows in enumerate((mine0, mine1)):
        other = swapped[t, :, HALF_FEAT:].astype(jnp.float32)
        own = (mine[t] + low[t].astype(jnp.float32)).astype(jnp.bfloat16)
        far = (other + high[t].astype(jnp.float32)).astype(jnp.bfloat16)
        left, right = jnp.where(swap, far, own), jnp.where(swap, own, far)
        for out, at in ((keys_out, 0), (values_out, HALF_KV)):
            out[0, t, :, :HALF_KV] = left[:, at : at + HALF_KV]
            out[0, t, :, HALF_KV:] = right[:, at : at + HALF_KV]
        near, far = rows[0], swapped[t, :, :HALF_FEAT]
        rows_out[0, t, :, :HALF_FEAT] = jnp.where(swap, far, near)
        rows_out[0, t, :, HALF_FEAT:] = jnp.where(swap, near, far)


def body(inputs, saved_keys, saved_values, query_gain, first_grads, head_grads, window, stride):
    index = lax.axis_index("ctx")
    section = lax.axis_index("pp")
    last = lax.axis_size("pp") - 1
    core = index % 2
    place = (index // 2) % 4
    f32, bf16 = jnp.float32, jnp.bfloat16

    def ctx(array, move, when=lambda i: True):
        return route(array, "ctx", lambda i: move(i) if when(i) else None)

    spot = index.astype(jnp.int32).reshape(1)
    half = shape((2, BLK, WIDE), bf16)
    ten = shape((10, BLK, WIDE), bf16)
    keep, give, kv_keep, kv_give = simple(
        split_all,
        [ten, ten, half, half],
        [spot, saved_keys, saved_values, inputs, first_grads, head_grads],
        far=True,
    )
    recv = sibling(give)
    up_low = ctx(kv_keep, lambda i: i + 8, lambda i: i % STRIDE == 0)
    up_high = ctx(kv_give, lambda i: i + 9, lambda i: i % STRIDE == 0)
    (pair,) = simple(pair_keys, [shape((2, 2 * BLK, WIDE), bf16)], [spot, keep, recv])
    pairs = [pair] + [ctx(pair, lambda i: i + 2 * d) for d in range(1, 4)]
    (start,) = simple(first_block, [half], [spot, keep, recv, up_low, up_high])
    across = []
    for d in range(1, 4):
        sent = start
        if d == 1:
            sent, pairs[1] = lax.optimization_barrier((start, pairs[1]))
        across.append(ctx(sent, lambda i: i + 2 * d, lambda i: (i // 2) % 4 == 0))
    (chosen,) = simple(choose, [half], [spot, start] + across)
    strided = [chosen]
    for s in range(1, 4):
        sent = chosen
        if s == 1:
            sent, pairs = lax.optimization_barrier((chosen, pairs))
        strided.append(ctx(sent, lambda i: i + STRIDE * s))
    gain = jnp.where(core == 0, query_gain[:, :HALF_FEAT], query_gain[:, HALF_FEAT:])
    heads = jnp.where(core == 0, window[0, :2], window[0, 2:])
    steps = jnp.where(core == 0, stride[0, :2], stride[0, 2:])
    top = jnp.where(section == last, 1, 0)
    meta = jnp.concatenate([jnp.stack([index, top]).astype(jnp.int32), heads, steps])

    first = attention(0, meta, gain, keep, recv, None, pairs, strided, None)
    grads = route(first[0], "pp", lambda i: i - 1)
    second = attention(1, meta, gain, keep, recv, grads, pairs, strided, first[1:8])
    backs = [ctx(second[1 + d], lambda i: i - 2 * d) for d in range(1, 4)]
    columns = [first[9], second[9]]
    for s in range(1, 4):
        sent = second[4 + s]
        if s == 1:
            sent, backs[0] = lax.optimization_barrier((sent, backs[0]))
        columns.append(ctx(sent, lambda i: i - STRIDE * s))

    wide = shape((2, BLK, WIDE), f32)
    total, send = simple(column_sum, [wide, half], columns, 0)
    rows = []
    for d in range(1, 4):
        sent = send
        if d == 1:
            sent, backs = lax.optimization_barrier((send, backs))
        rows.append(ctx(sent, lambda i: i - 2 * d, lambda i: (i // 2) % 4 == d))
    mine, swap, down = simple(
        row_sum,
        [wide, shape((2, BLK, HALF_FEAT + WIDE), bf16), half],
        [spot, total] + rows + [first[8], second[8]] + backs + [second[1]],
    )
    swapped = sibling(swap)
    low = ctx(down, lambda i: i - 8, lambda i: i % STRIDE == 8)
    high = ctx(down, lambda i: i - 9, lambda i: i % STRIDE == 9)
    keys_shape = shape(saved_keys.shape, bf16)
    grads_out, key_grads, value_grads = simple(
        finish,
        [shape(inputs.shape, bf16), keys_shape, keys_shape],
        [spot, mine, swapped, low, high, first[0], second[0]],
    )
    return grads_out, key_grads, value_grads


def solution(mesh):
    in_specs = (
        P("pp", None, "ctx", None),
        P("pp", None, "ctx", None),
        P("pp", None, "ctx", None),
        P("pp", None),
        P("pp", "ctx", None),
        P(None, "ctx", None),
        P("pp", None),
        P("pp", None),
    )
    out_specs = (P("pp", None, "ctx", None), P("pp", None, "ctx", None), P("pp", None, "ctx", None))
    return jax.shard_map(body, mesh=mesh, in_specs=in_specs, out_specs=out_specs, check_vma=False)
```

```python
import functools

import jax
import jax.numpy as jnp
from jax import lax
from jax.experimental import pallas as pl
from jax.experimental.pallas import tpu as pltpu
from jax.sharding import PartitionSpec as P

BLK = 64
WIN = 7
STRIDE = 16
HEAD_DIM = 128
GROUP = 4
HALF_HEADS = 2
HALF_KV = HALF_HEADS * HEAD_DIM
HALF_FEAT = HALF_HEADS * GROUP * HEAD_DIM
SCALE = HEAD_DIM**-0.5
TA = 3
TB = 2
LOG2E = 1.4426950408889634
NEG = -1e30
NT = (((1,), (1,)), ((), ()))
TN = (((0,), (0,)), ((), ()))


def route(array, axis, move):
    size = lax.axis_size(axis)
    pairs = [(i, move(i)) for i in range(size)]
    return lax.ppermute(array, axis, [(a, b) for a, b in pairs if b is not None and 0 <= b < size])


def sibling(array):
    return route(array, "ctx", lambda i: i ^ 1)


def attention_kernel(tick, meta, gain, keep, recv, *refs):
    if tick:
        grads, refs = refs[0], refs[1:]
    pairs, strided = refs[:4], refs[4:8]
    refs = refs[8:]
    if tick:
        for old, new in zip(refs[:7], refs[8:15]):
            new[0] = old[...]
        refs = refs[7:]
        refs = refs[:1] + tuple(r.at[1] for r in refs[1:8]) + refs[8:]
    both, other, back1, back2, back3, part1, part2, part3, own, part0 = refs
    backs = (own, back1, back2, back3)
    parts = (part0, part1, part2, part3)
    index = meta[0]
    blocks = (index, jnp.bitwise_xor(index, 1))
    group = index // STRIDE
    for h in range(HALF_HEADS):
        window = meta[2 + h]
        stride = meta[4 + h]
        q_rows, g_rows = [], []
        for half, source in enumerate((keep, recv)):
            for j in range(GROUP):
                near = slice(j * HEAD_DIM, (j + 1) * HEAD_DIM)
                at = slice((h * GROUP + j) * HEAD_DIM, (h * GROUP + j + 1) * HEAD_DIM)
                rows = source[2 + 2 * tick + h, :, near].astype(jnp.float32)
                q_rows.append((rows * gain[:, at]).astype(jnp.bfloat16))
                if tick:
                    top = source[8 + h, :, near]
                    g_rows.append(jnp.where(meta[1] == 1, top, grads[half, :, at]))
                else:
                    g_rows.append(source[6 + h, :, near])
        q = jnp.concatenate(q_rows, axis=0)
        g = jnp.concatenate(g_rows, axis=0)
        k_at = slice(h * HEAD_DIM, (h + 1) * HEAD_DIM)
        v_at = slice(HALF_KV + h * HEAD_DIM, HALF_KV + (h + 1) * HEAD_DIM)
        k = jnp.concatenate([r[:, k_at] for r in pairs + strided], axis=0)
        v = jnp.concatenate([r[:, v_at] for r in pairs + strided], axis=0)
        scores = lax.dot_general(k, q, NT, preferred_element_type=jnp.float32)
        wide = GROUP * BLK
        key_row = lax.broadcasted_iota(jnp.int32, (BLK, wide), 0)
        query_row = lax.broadcasted_iota(jnp.int32, (BLK, wide), 1) % BLK
        rows = []
        for slot in range(12):
            cells = []
            for half in range(2):
                query_block = blocks[half]
                if slot < 8:
                    key_block = blocks[slot % 2] - 2 * (slot // 2)
                    gap = query_block - key_block
                    ok = (key_block >= 0) & (gap >= 0) & (gap < WIN)
                    ok = ok & ((gap < window) | (key_block % stride == 0))
                else:
                    key_block = STRIDE * (group - (slot - 8))
                    ok = (key_block >= 0) & (key_block <= query_block - WIN)
                    ok = ok & (key_block % stride == 0)
                cell = scores[slot * BLK : (slot + 1) * BLK, half * wide : (half + 1) * wide]
                if slot == half:
                    cell = jnp.where(key_row <= query_row, cell, NEG)
                else:
                    cell = jnp.where(ok, cell, NEG)
                cells.append(cell)
            rows.append(jnp.concatenate(cells, axis=1))
        scores = jnp.concatenate(rows, axis=0)
        peak = jnp.max(scores, axis=0, keepdims=True)
        weights = jnp.exp2((scores - peak) * (SCALE * LOG2E))
        probs = weights * (1.0 / jnp.sum(weights, axis=0, keepdims=True))
        grad_prob = lax.dot_general(v, g, NT, preferred_element_type=jnp.float32)
        delta = jnp.sum(probs * grad_prob, axis=0, keepdims=True)
        dscore = (probs * (grad_prob - delta)).astype(jnp.bfloat16)
        dquery = lax.dot_general(dscore, k, TN, preferred_element_type=jnp.float32) * SCALE
        dkey = jnp.dot(dscore, q, preferred_element_type=jnp.float32) * SCALE
        dvalue = jnp.dot(probs.astype(jnp.bfloat16), g, preferred_element_type=jnp.float32)
        for half in range(2):
            for j in range(GROUP):
                at = slice((h * GROUP + j) * HEAD_DIM, (h * GROUP + j + 1) * HEAD_DIM)
                row = (half * GROUP + j) * BLK
                grad = g[row : row + BLK].astype(jnp.float32)
                total = grad + gain[:, at] * dquery[row : row + BLK]
                total = total.astype(jnp.bfloat16)
                both[half, :, at] = total
                if half == 1:
                    other[:, at] = total
        for d in range(4):
            rows_at = slice(2 * BLK * d, 2 * BLK * (d + 1))
            backs[d][:, k_at] = dkey[rows_at].astype(backs[d].dtype)
            backs[d][:, v_at] = dvalue[rows_at].astype(backs[d].dtype)
        for s in range(4):
            rows_at = slice(8 * BLK + BLK * s, 8 * BLK + BLK * (s + 1))
            parts[s][:, k_at] = dkey[rows_at].astype(parts[s].dtype)
            parts[s][:, v_at] = dvalue[rows_at].astype(parts[s].dtype)


WHOLE = pl.BlockSpec(memory_space=pltpu.VMEM)
FAR = pl.BlockSpec(memory_space=pltpu.HBM)
SCALAR = pl.BlockSpec(memory_space=pltpu.SMEM)
WIDE = 2 * HALF_KV


def shape(dims, dtype):
    return jax.ShapeDtypeStruct(dims, dtype)


def attention(tick, meta, gain, keep, recv, grads, pairs, strided, earlier):
    def at(lead, *rest):
        return pl.BlockSpec((None,) + rest, lambda n: (lead, 0, 0))

    args = [meta, gain, keep, recv]
    specs = [SCALAR, WHOLE, WHOLE, WHOLE]
    if tick:
        args.append(grads)
        specs.append(WHOLE)
    args += list(pairs) + list(strided)
    specs += [at(tick, 2 * BLK, WIDE)] * 4 + [at(tick, BLK, WIDE)] * 4
    bf16, f32 = jnp.bfloat16, jnp.float32
    out_shape = [shape((2, BLK, HALF_FEAT), bf16)]
    lead = (2,) if tick else ()
    if tick:
        args += earlier
        specs += [WHOLE] * 7
    out_shape.append(shape(lead + (BLK, HALF_FEAT), bf16))
    out_shape += [shape(lead + (2 * BLK, WIDE), bf16)] * 3
    out_shape += [shape(lead + (BLK, WIDE), bf16)] * 3
    out_shape += [shape((2 * BLK, WIDE), f32), shape((BLK, WIDE), f32)]
    return pl.pallas_call(
        functools.partial(attention_kernel, tick),
        out_shape=out_shape,
        grid=(1,),
        in_specs=specs,
        out_specs=[WHOLE] * len(out_shape),
        compiler_params=pltpu.CompilerParams(vmem_limit_bytes=32 << 20),
        cost_estimate=pl.CostEstimate(
            flops=2 * 5 * 2 * 512 * 768 * 128, bytes_accessed=4 << 20, transcendentals=2 * 512 * 768
        ),
        name="attention",
    )(*args)


def far_scratch(arrays):
    buffers = [pltpu.VMEM(a.shape, a.dtype) for a in arrays]
    return buffers + [pltpu.SemaphoreType.DMA((len(arrays),))]


def simple(kernel, out_shape, args, scalars=1, far=False):
    size = sum(a.size * a.dtype.itemsize for a in list(args) + list(out_shape))
    return pl.pallas_call(
        kernel,
        out_shape=out_shape,
        in_specs=[SCALAR] * scalars + [FAR if far else WHOLE] * (len(args) - scalars),
        out_specs=[WHOLE] * len(out_shape),
        scratch_shapes=far_scratch(args[scalars:]) if far else [],
        compiler_params=pltpu.CompilerParams(vmem_limit_bytes=(56 if far else 16) << 20),
        cost_estimate=pl.CostEstimate(flops=size, bytes_accessed=size, transcendentals=0),
        name=kernel.__name__,
    )(*args)


def column_sum(own0, own1, x1, x2, x3, wide_out, send_out):
    for t, own in enumerate((own0, own1)):
        total = own[...]
        for x in (x1, x2, x3):
            total = total + x[t].astype(jnp.float32)
        wide_out[t] = total
        send_out[t] = total.astype(jnp.bfloat16)


def split_all(meta, *refs):
    sources, (keep, give, kv_keep, kv_give), buffers, sems = refs[:5], refs[5:9], refs[9:14], refs[14]
    copies = [
        pltpu.make_async_copy(source, buffer, sems.at[n])
        for n, (source, buffer) in enumerate(zip(sources, buffers))
    ]
    for copy in copies:
        copy.start()
    for copy in copies:
        copy.wait()
    keys, values, inputs, first, head = buffers
    swap = meta[0] % 2 == 1
    for source, at in ((keys, 0), (values, HALF_KV)):
        low, high = source[0, :, :, :HALF_KV], source[0, :, :, HALF_KV:]
        mine, far = jnp.where(swap, high, low), jnp.where(swap, low, high)
        keep[:2, :, at : at + HALF_KV] = mine
        give[:2, :, at : at + HALF_KV] = far
        kv_keep[:, :, at : at + HALF_KV] = mine
        kv_give[:, :, at : at + HALF_KV] = far
    for n, source in enumerate((inputs.at[0, 0], inputs.at[0, 1], first.at[0], head.at[0])):
        for h in range(HALF_HEADS):
            low = source[:, h * WIDE : (h + 1) * WIDE]
            high = source[:, HALF_FEAT + h * WIDE : HALF_FEAT + (h + 1) * WIDE]
            keep[2 + 2 * n + h] = jnp.where(swap, high, low)
            give[2 + 2 * n + h] = jnp.where(swap, low, high)


def pair_keys(meta, keep, recv, up_low, up_high, pair, start):
    keep, recv = keep.at[:2], recv.at[:2]
    core = meta[0] % 2
    even = (meta[0] // 8) % 2 == 0
    pair[:, :BLK] = keep[...]
    pair[:, BLK:] = recv[...]
    near = jnp.where(core == 0, keep[...], recv[...])
    above = jnp.where(core == 0, up_low[...], up_high[...])
    start[...] = jnp.where(even, near, above)


def choose(meta, start, x1, x2, x3, out):
    place = (meta[0] // 2) % 4
    near = jnp.where(place == 0, start[...], x1[...])
    far = jnp.where(place == 2, x2[...], x3[...])
    out[...] = jnp.where(place < 2, near, far)


def row_sum(meta, *refs):
    total, x1, x2, x3, own0, own1, back1, back2, back3, far_rows = refs[:10]
    mine_out, swap_out, strided_out = refs[10:]
    index = meta[0]
    owner = (index // 2) % 4 == 0
    even = (index // 8) % 2 == 0
    first = (owner & even & (index % 2 == 0)).astype(jnp.float32)
    second = (owner & even & (index % 2 == 1)).astype(jnp.float32)
    for t, own in enumerate((own0, own1)):
        strided = total[t]
        for x in (x1, x2, x3):
            strided = strided + x[t].astype(jnp.float32)
        strided_out[t] = strided.astype(jnp.bfloat16)
        near = own[...]
        for back in (back1, back2, back3):
            near = near + back[t].astype(jnp.float32)
        mine_out[t] = near[:BLK] + first * strided
        swap_out[t, :, :HALF_FEAT] = far_rows[t]
        swap_out[t, :, HALF_FEAT:] = (near[BLK:] + second * strided).astype(jnp.bfloat16)


def finish(meta, mine, swapped, low, high, mine0, mine1, rows_out, keys_out, values_out):
    swap = meta[0] % 2 == 1
    for t, rows in enumerate((mine0, mine1)):
        other = swapped[t, :, HALF_FEAT:].astype(jnp.float32)
        own = (mine[t] + low[t].astype(jnp.float32)).astype(jnp.bfloat16)
        far = (other + high[t].astype(jnp.float32)).astype(jnp.bfloat16)
        left, right = jnp.where(swap, far, own), jnp.where(swap, own, far)
        for out, at in ((keys_out, 0), (values_out, HALF_KV)):
            out[0, t, :, :HALF_KV] = left[:, at : at + HALF_KV]
            out[0, t, :, HALF_KV:] = right[:, at : at + HALF_KV]
        near, far = rows[0], swapped[t, :, :HALF_FEAT]
        rows_out[0, t, :, :HALF_FEAT] = jnp.where(swap, far, near)
        rows_out[0, t, :, HALF_FEAT:] = jnp.where(swap, near, far)


def body(inputs, saved_keys, saved_values, query_gain, first_grads, head_grads, window, stride):
    index = lax.axis_index("ctx")
    section = lax.axis_index("pp")
    last = lax.axis_size("pp") - 1
    core = index % 2
    place = (index // 2) % 4
    f32, bf16 = jnp.float32, jnp.bfloat16

    def ctx(array, move, when=lambda i: True):
        return route(array, "ctx", lambda i: move(i) if when(i) else None)

    spot = index.astype(jnp.int32).reshape(1)
    half = shape((2, BLK, WIDE), bf16)
    ten = shape((10, BLK, WIDE), bf16)
    keep, give, kv_keep, kv_give = simple(
        split_all,
        [ten, ten, half, half],
        [spot, saved_keys, saved_values, inputs, first_grads, head_grads],
        far=True,
    )
    recv = sibling(give)
    up_low = ctx(kv_keep, lambda i: i + 8, lambda i: i % STRIDE == 0)
    up_high = ctx(kv_give, lambda i: i + 9, lambda i: i % STRIDE == 0)
    pair, start = simple(
        pair_keys,
        [shape((2, 2 * BLK, WIDE), bf16), half],
        [spot, keep, recv, up_low, up_high],
    )
    across = [ctx(start, lambda i: i + 2 * d, lambda i: (i // 2) % 4 == 0) for d in range(1, 4)]
    (chosen,) = simple(choose, [half], [spot, start] + across)
    pairs = [pair] + [ctx(pair, lambda i: i + 2 * d) for d in range(1, 4)]
    strided = [chosen]
    for s in range(1, 4):
        sent = chosen
        if s == 1:
            sent, pairs[TA] = lax.optimization_barrier((chosen, pairs[TA]))
        strided.append(ctx(sent, lambda i: i + STRIDE * s))

    gain = jnp.where(core == 0, query_gain[:, :HALF_FEAT], query_gain[:, HALF_FEAT:])
    heads = jnp.where(core == 0, window[0, :2], window[0, 2:])
    steps = jnp.where(core == 0, stride[0, :2], stride[0, 2:])
    top = jnp.where(section == last, 1, 0)
    meta = jnp.concatenate([jnp.stack([index, top]).astype(jnp.int32), heads, steps])

    first = attention(0, meta, gain, keep, recv, None, pairs, strided, None)
    grads = route(first[0], "pp", lambda i: i - 1)
    second = attention(1, meta, gain, keep, recv, grads, pairs, strided, first[1:8])
    columns = [first[9], second[9]]
    columns += [ctx(second[4 + s], lambda i: i - STRIDE * s) for s in range(1, 4)]
    backs = [ctx(second[1 + d], lambda i: i - 2 * d) for d in range(1, 4)]

    wide = shape((2, BLK, WIDE), f32)
    total, send = simple(column_sum, [wide, half], columns, 0)
    rows = []
    for d in range(1, 4):
        sent = send
        if d == 1:
            sent, backs[TB] = lax.optimization_barrier((send, backs[TB]))
        rows.append(ctx(sent, lambda i: i - 2 * d, lambda i: (i // 2) % 4 == d))
    mine, swap, down = simple(
        row_sum,
        [wide, shape((2, BLK, HALF_FEAT + WIDE), bf16), half],
        [spot, total] + rows + [first[8], second[8]] + backs + [second[1]],
    )
    swapped = sibling(swap)
    low = ctx(down, lambda i: i - 8, lambda i: i % STRIDE == 8)
    high = ctx(down, lambda i: i - 9, lambda i: i % STRIDE == 9)
    keys_shape = shape(saved_keys.shape, bf16)
    grads_out, key_grads, value_grads = simple(
        finish,
        [shape(inputs.shape, bf16), keys_shape, keys_shape],
        [spot, mine, swapped, low, high, first[0], second[0]],
    )
    return grads_out, key_grads, value_grads


def solution(mesh):
    in_specs = (
        P("pp", None, "ctx", None),
        P("pp", None, "ctx", None),
        P("pp", None, "ctx", None),
        P("pp", None),
        P("pp", "ctx", None),
        P(None, "ctx", None),
        P("pp", None),
        P("pp", None),
    )
    out_specs = (P("pp", None, "ctx", None), P("pp", None, "ctx", None), P("pp", None, "ctx", None))
    return jax.shard_map(body, mesh=mesh, in_specs=in_specs, out_specs=out_specs, check_vma=False)
```

```python
import functools

import jax
import jax.numpy as jnp
from jax import lax
from jax.experimental import pallas as pl
from jax.experimental.pallas import tpu as pltpu
from jax.sharding import PartitionSpec as P

BLK = 64
WIN = 7
STRIDE = 16
HEAD_DIM = 128
GROUP = 4
HALF_HEADS = 2
HALF_KV = HALF_HEADS * HEAD_DIM
HALF_FEAT = HALF_HEADS * GROUP * HEAD_DIM
SCALE = HEAD_DIM**-0.5
LOG2E = 1.4426950408889634
NEG = -1e30
NT = (((1,), (1,)), ((), ()))
TN = (((0,), (0,)), ((), ()))


def route(array, axis, move):
    size = lax.axis_size(axis)
    pairs = [(i, move(i)) for i in range(size)]
    return lax.ppermute(array, axis, [(a, b) for a, b in pairs if b is not None and 0 <= b < size])


def sibling(array):
    return route(array, "ctx", lambda i: i ^ 1)


def attention_kernel(has_head, *refs):
    meta, gain, q_mine, q_other, g_mine, g_other = refs[:6]
    refs = refs[6:]
    if has_head:
        h_mine, h_other = refs[:2]
        refs = refs[2:]
    pairs, strided = refs[:4], refs[4:8]
    refs = refs[8:]
    if has_head:
        for old, new in zip(refs[:4], refs[5:9]):
            new[0] = old[...]
        refs = refs[4:]
        refs = refs[:1] + tuple(r.at[1] for r in refs[1:5]) + refs[5:]
    both, other, back1, back2, back3, own, part0, part1, part2, part3 = refs
    backs = (own, back1, back2, back3)
    parts = (part0, part1, part2, part3)
    index = meta[0]
    blocks = (index, jnp.bitwise_xor(index, 1))
    group = index // STRIDE
    for h in range(HALF_HEADS):
        window = meta[2 + h]
        stride = meta[4 + h]
        q_rows, g_rows = [], []
        for half, (q_ref, g_ref) in enumerate(((q_mine, g_mine), (q_other, g_other))):
            for j in range(GROUP):
                at = slice((h * GROUP + j) * HEAD_DIM, (h * GROUP + j + 1) * HEAD_DIM)
                q_rows.append((q_ref[:, at].astype(jnp.float32) * gain[:, at]).astype(jnp.bfloat16))
                grad = g_ref[:, at]
                if has_head:
                    top = (h_mine, h_other)[half][:, at]
                    grad = jnp.where(meta[1] == 1, top, grad)
                g_rows.append(grad)
        q = jnp.concatenate(q_rows, axis=0)
        g = jnp.concatenate(g_rows, axis=0)
        k_at = slice(h * HEAD_DIM, (h + 1) * HEAD_DIM)
        v_at = slice(HALF_KV + h * HEAD_DIM, HALF_KV + (h + 1) * HEAD_DIM)
        k = jnp.concatenate([r[:, k_at] for r in pairs + strided], axis=0)
        v = jnp.concatenate([r[:, v_at] for r in pairs + strided], axis=0)
        scores = lax.dot_general(k, q, NT, preferred_element_type=jnp.float32)
        wide = GROUP * BLK
        key_row = lax.broadcasted_iota(jnp.int32, (BLK, wide), 0)
        query_row = lax.broadcasted_iota(jnp.int32, (BLK, wide), 1) % BLK
        rows = []
        for slot in range(12):
            cells = []
            for half in range(2):
                query_block = blocks[half]
                if slot < 8:
                    key_block = blocks[slot % 2] - 2 * (slot // 2)
                    gap = query_block - key_block
                    ok = (key_block >= 0) & (gap >= 0) & (gap < WIN)
                    ok = ok & ((gap < window) | (key_block % stride == 0))
                else:
                    key_block = STRIDE * (group - (slot - 8))
                    ok = (key_block >= 0) & (key_block <= query_block - WIN)
                    ok = ok & (key_block % stride == 0)
                cell = scores[slot * BLK : (slot + 1) * BLK, half * wide : (half + 1) * wide]
                if slot == half:
                    cell = jnp.where(key_row <= query_row, cell, NEG)
                else:
                    cell = jnp.where(ok, cell, NEG)
                cells.append(cell)
            rows.append(jnp.concatenate(cells, axis=1))
        scores = jnp.concatenate(rows, axis=0)
        peak = jnp.max(scores, axis=0, keepdims=True)
        weights = jnp.exp2((scores - peak) * (SCALE * LOG2E))
        probs = weights * (1.0 / jnp.sum(weights, axis=0, keepdims=True))
        grad_prob = lax.dot_general(v, g, NT, preferred_element_type=jnp.float32)
        delta = jnp.sum(probs * grad_prob, axis=0, keepdims=True)
        dscore = (probs * (grad_prob - delta)).astype(jnp.bfloat16)
        dquery = lax.dot_general(dscore, k, TN, preferred_element_type=jnp.float32) * SCALE
        dkey = jnp.dot(dscore, q, preferred_element_type=jnp.float32) * SCALE
        dvalue = jnp.dot(probs.astype(jnp.bfloat16), g, preferred_element_type=jnp.float32)
        for half in range(2):
            for j in range(GROUP):
                at = slice((h * GROUP + j) * HEAD_DIM, (h * GROUP + j + 1) * HEAD_DIM)
                row = (half * GROUP + j) * BLK
                grad = g[row : row + BLK].astype(jnp.float32)
                total = grad + gain[:, at] * dquery[row : row + BLK]
                total = total.astype(jnp.bfloat16)
                both[half, :, at] = total
                if half == 1:
                    other[:, at] = total
        for d in range(4):
            rows_at = slice(2 * BLK * d, 2 * BLK * (d + 1))
            backs[d][:, k_at] = dkey[rows_at].astype(backs[d].dtype)
            backs[d][:, v_at] = dvalue[rows_at].astype(backs[d].dtype)
        for s in range(4):
            rows_at = slice(8 * BLK + BLK * s, 8 * BLK + BLK * (s + 1))
            parts[s][:, k_at] = dkey[rows_at].astype(parts[s].dtype)
            parts[s][:, v_at] = dvalue[rows_at].astype(parts[s].dtype)


WHOLE = pl.BlockSpec(memory_space=pltpu.VMEM)
SCALAR = pl.BlockSpec(memory_space=pltpu.SMEM)
WIDE = 2 * HALF_KV


def shape(dims, dtype):
    return jax.ShapeDtypeStruct(dims, dtype)


def attention(tick, meta, gain, keep, recv, grads, pairs, strided, earlier):
    def at(lead, *rest):
        return pl.BlockSpec((None,) + rest, lambda n: (lead, 0, 0))

    args = [meta, gain, keep, recv]
    specs = [SCALAR, WHOLE, at(tick, BLK, HALF_FEAT), at(tick, BLK, HALF_FEAT)]
    if grads is None:
        args += [keep, recv]
        specs += [at(2, BLK, HALF_FEAT), at(2, BLK, HALF_FEAT)]
    else:
        args += [grads, grads, keep, recv]
        specs += [at(0, BLK, HALF_FEAT), at(1, BLK, HALF_FEAT)]
        specs += [at(3, BLK, HALF_FEAT), at(3, BLK, HALF_FEAT)]
    args += list(pairs) + list(strided)
    specs += [at(tick, 2 * BLK, WIDE)] * 4 + [at(tick, BLK, WIDE)] * 4
    bf16, f32 = jnp.bfloat16, jnp.float32
    out_shape = [shape((2, BLK, HALF_FEAT), bf16)]
    if earlier is None:
        out_shape += [shape((BLK, HALF_FEAT), bf16)] + [shape((2 * BLK, WIDE), bf16)] * 3
    else:
        args += earlier
        specs += [WHOLE] * 4
        out_shape += [shape((2, BLK, HALF_FEAT), bf16)] + [shape((2, 2 * BLK, WIDE), bf16)] * 3
    out_shape += [shape((2 * BLK, WIDE), f32), shape((BLK, WIDE), f32)]
    out_shape += [shape((BLK, WIDE), bf16)] * 3
    return pl.pallas_call(
        functools.partial(attention_kernel, grads is not None),
        out_shape=out_shape,
        grid=(1,),
        in_specs=specs,
        out_specs=[WHOLE] * len(out_shape),
        compiler_params=pltpu.CompilerParams(vmem_limit_bytes=32 << 20),
        cost_estimate=pl.CostEstimate(
            flops=2 * 5 * 2 * 512 * 768 * 128, bytes_accessed=4 << 20, transcendentals=2 * 512 * 768
        ),
        name="attention",
    )(*args)


def simple(kernel, out_shape, args, scalars=1):
    size = sum(a.size * a.dtype.itemsize for a in list(args) + list(out_shape))
    return pl.pallas_call(
        kernel,
        out_shape=out_shape,
        in_specs=[SCALAR] * scalars + [WHOLE] * (len(args) - scalars),
        out_specs=[WHOLE] * len(out_shape),
        compiler_params=pltpu.CompilerParams(vmem_limit_bytes=16 << 20),
        cost_estimate=pl.CostEstimate(flops=size, bytes_accessed=size, transcendentals=0),
        name=kernel.__name__,
    )(*args)


def column_sum(*refs):
    wide_out, send_out = refs[8:]
    for t in range(2):
        total = refs[4 * t][...]
        for s in range(1, 4):
            total = total + refs[4 * t + s][...].astype(jnp.float32)
        wide_out[t] = total
        send_out[t] = total.astype(jnp.bfloat16)


def split_keys(meta, keys, values, keep, give):
    swap = meta[0] % 2 == 1
    for source, at in ((keys, 0), (values, HALF_KV)):
        low, high = source[0, :, :, :HALF_KV], source[0, :, :, HALF_KV:]
        keep[:, :, at : at + HALF_KV] = jnp.where(swap, high, low)
        give[:, :, at : at + HALF_KV] = jnp.where(swap, low, high)


def split_rows(meta, inputs, first, head, keep, give):
    swap = meta[0] % 2 == 1
    for n, source in enumerate((inputs.at[0, 0], inputs.at[0, 1], first.at[0], head.at[0])):
        low, high = source[:, :HALF_FEAT], source[:, HALF_FEAT:]
        keep[n] = jnp.where(swap, high, low)
        give[n] = jnp.where(swap, low, high)


def pair_keys(meta, keep, recv, up_low, up_high, pair, start):
    core = meta[0] % 2
    even = (meta[0] // 8) % 2 == 0
    pair[:, :BLK] = keep[...]
    pair[:, BLK:] = recv[...]
    near = jnp.where(core == 0, keep[...], recv[...])
    above = jnp.where(core == 0, up_low[...], up_high[...])
    start[...] = jnp.where(even, near, above)


def row_sum(meta, *refs):
    total, x1, x2, x3, own0, own1, back1, back2, back3, far_rows = refs[:10]
    mine_out, swap_out, strided_out = refs[10:]
    index = meta[0]
    owner = (index // 2) % 4 == 0
    even = (index // 8) % 2 == 0
    first = (owner & even & (index % 2 == 0)).astype(jnp.float32)
    second = (owner & even & (index % 2 == 1)).astype(jnp.float32)
    for t, own in enumerate((own0, own1)):
        strided = total[t]
        for x in (x1, x2, x3):
            strided = strided + x[t].astype(jnp.float32)
        strided_out[t] = strided.astype(jnp.bfloat16)
        near = own[...]
        for back in (back1, back2, back3):
            near = near + back[t].astype(jnp.float32)
        mine_out[t] = near[:BLK] + first * strided
        swap_out[t, :, :HALF_FEAT] = far_rows[t]
        swap_out[t, :, HALF_FEAT:] = (near[BLK:] + second * strided).astype(jnp.bfloat16)


def finish(meta, mine, swapped, low, high, mine0, mine1, rows_out, keys_out, values_out):
    swap = meta[0] % 2 == 1
    for t, rows in enumerate((mine0, mine1)):
        other = swapped[t, :, HALF_FEAT:].astype(jnp.float32)
        own = (mine[t] + low[t].astype(jnp.float32)).astype(jnp.bfloat16)
        far = (other + high[t].astype(jnp.float32)).astype(jnp.bfloat16)
        left, right = jnp.where(swap, far, own), jnp.where(swap, own, far)
        for out, at in ((keys_out, 0), (values_out, HALF_KV)):
            out[0, t, :, :HALF_KV] = left[:, at : at + HALF_KV]
            out[0, t, :, HALF_KV:] = right[:, at : at + HALF_KV]
        near, far = rows[0], swapped[t, :, :HALF_FEAT]
        rows_out[0, t, :, :HALF_FEAT] = jnp.where(swap, far, near)
        rows_out[0, t, :, HALF_FEAT:] = jnp.where(swap, near, far)


def body(inputs, saved_keys, saved_values, query_gain, first_grads, head_grads, window, stride):
    index = lax.axis_index("ctx")
    section = lax.axis_index("pp")
    last = lax.axis_size("pp") - 1
    core = index % 2
    place = (index // 2) % 4
    f32, bf16 = jnp.float32, jnp.bfloat16

    def ctx(array, move, when=lambda i: True):
        return route(array, "ctx", lambda i: move(i) if when(i) else None)

    spot = index.astype(jnp.int32).reshape(1)
    half = shape((2, BLK, WIDE), bf16)
    kv_keep, kv_give = simple(split_keys, [half, half], [spot, saved_keys, saved_values])
    kv_recv = sibling(kv_give)
    up_low = ctx(kv_keep, lambda i: i + 8, lambda i: i % STRIDE == 0)
    up_high = ctx(kv_give, lambda i: i + 9, lambda i: i % STRIDE == 0)
    pair, start = simple(
        pair_keys,
        [shape((2, 2 * BLK, WIDE), bf16), half],
        [spot, kv_keep, kv_recv, up_low, up_high],
    )
    chosen = start
    for d in range(1, 4):
        across = ctx(start, lambda i: i + 2 * d, lambda i: (i // 2) % 4 == 0)
        chosen = jnp.where(place == d, across, chosen)
    pairs = [pair] + [ctx(pair, lambda i: i + 2 * d) for d in range(1, 4)]
    strided = [chosen] + [ctx(chosen, lambda i: i + STRIDE * s) for s in range(1, 4)]

    four = shape((4, BLK, HALF_FEAT), bf16)
    keep, give = simple(split_rows, [four, four], [spot, inputs, first_grads, head_grads])
    recv = sibling(give)
    gain = jnp.where(core == 0, query_gain[:, :HALF_FEAT], query_gain[:, HALF_FEAT:])
    heads = jnp.where(core == 0, window[0, :2], window[0, 2:])
    steps = jnp.where(core == 0, stride[0, :2], stride[0, 2:])
    top = jnp.where(section == last, 1, 0)
    meta = jnp.concatenate([jnp.stack([index, top]).astype(jnp.int32), heads, steps])

    first = attention(0, meta, gain, keep, recv, None, pairs, strided, None)
    grads = route(first[0], "pp", lambda i: i - 1)
    second = attention(1, meta, gain, keep, recv, grads, pairs, strided, first[1:5])
    columns = []
    for outs in (first, second):
        columns.append(outs[6])
        columns += [ctx(outs[6 + s], lambda i: i - STRIDE * s) for s in range(1, 4)]
    backs = [ctx(second[1 + d], lambda i: i - 2 * d) for d in range(1, 4)]

    wide = shape((2, BLK, WIDE), f32)
    total, send = simple(column_sum, [wide, half], columns, 0)
    rows = [ctx(send, lambda i: i - 2 * d, lambda i: (i // 2) % 4 == d) for d in range(1, 4)]
    mine, swap, down = simple(
        row_sum,
        [wide, shape((2, BLK, HALF_FEAT + WIDE), bf16), half],
        [spot, total] + rows + [first[5], second[5]] + backs + [second[1]],
    )
    swapped = sibling(swap)
    low = ctx(down, lambda i: i - 8, lambda i: i % STRIDE == 8)
    high = ctx(down, lambda i: i - 9, lambda i: i % STRIDE == 9)
    keys_shape = shape(saved_keys.shape, bf16)
    grads_out, key_grads, value_grads = simple(
        finish,
        [shape(inputs.shape, bf16), keys_shape, keys_shape],
        [spot, mine, swapped, low, high, first[0], second[0]],
    )
    return grads_out, key_grads, value_grads


def solution(mesh):
    in_specs = (
        P("pp", None, "ctx", None),
        P("pp", None, "ctx", None),
        P("pp", None, "ctx", None),
        P("pp", None),
        P("pp", "ctx", None),
        P(None, "ctx", None),
        P("pp", None),
        P("pp", None),
    )
    out_specs = (P("pp", None, "ctx", None), P("pp", None, "ctx", None), P("pp", None, "ctx", None))
    return jax.shard_map(body, mesh=mesh, in_specs=in_specs, out_specs=out_specs, check_vma=False)
```

```python
import functools

import jax
import jax.numpy as jnp
from jax import lax
from jax.experimental import pallas as pl
from jax.experimental.pallas import tpu as pltpu
from jax.sharding import PartitionSpec as P

BLK = 64
WIN = 7
STRIDE = 16
HEAD_DIM = 128
GROUP = 4
HALF_HEADS = 2
HALF_KV = HALF_HEADS * HEAD_DIM
HALF_FEAT = HALF_HEADS * GROUP * HEAD_DIM
SCALE = HEAD_DIM**-0.5
LOG2E = 1.4426950408889634
NEG = -1e30
NT = (((1,), (1,)), ((), ()))
TN = (((0,), (0,)), ((), ()))


def route(array, axis, move):
    size = lax.axis_size(axis)
    pairs = [(i, move(i)) for i in range(size)]
    return lax.ppermute(array, axis, [(a, b) for a, b in pairs if b is not None and 0 <= b < size])


def sibling(array):
    return route(array, "ctx", lambda i: i ^ 1)


def attention_kernel(has_head, *refs):
    meta, gain, q_mine, q_other, g_mine, g_other = refs[:6]
    refs = refs[6:]
    if has_head:
        h_mine, h_other = refs[:2]
        refs = refs[2:]
    pairs, strided = refs[:4], refs[4:8]
    refs = refs[8:]
    if has_head:
        for old, new in zip(refs[:4], refs[5:9]):
            new[0] = old[...]
        refs = refs[4:]
        refs = refs[:1] + tuple(r.at[1] for r in refs[1:5]) + refs[5:]
    both, other, back1, back2, back3, own, part0, part1, part2, part3 = refs
    backs = (own, back1, back2, back3)
    parts = (part0, part1, part2, part3)
    index = meta[0]
    blocks = (index, jnp.bitwise_xor(index, 1))
    group = index // STRIDE
    for h in range(HALF_HEADS):
        window = meta[2 + h]
        stride = meta[4 + h]
        q_rows, g_rows = [], []
        for half, (q_ref, g_ref) in enumerate(((q_mine, g_mine), (q_other, g_other))):
            for j in range(GROUP):
                at = slice((h * GROUP + j) * HEAD_DIM, (h * GROUP + j + 1) * HEAD_DIM)
                q_rows.append((q_ref[:, at].astype(jnp.float32) * gain[:, at]).astype(jnp.bfloat16))
                grad = g_ref[:, at]
                if has_head:
                    top = (h_mine, h_other)[half][:, at]
                    grad = jnp.where(meta[1] == 1, top, grad)
                g_rows.append(grad)
        q = jnp.concatenate(q_rows, axis=0)
        g = jnp.concatenate(g_rows, axis=0)
        k_at = slice(h * HEAD_DIM, (h + 1) * HEAD_DIM)
        v_at = slice(HALF_KV + h * HEAD_DIM, HALF_KV + (h + 1) * HEAD_DIM)
        k = jnp.concatenate([r[:, k_at] for r in pairs + strided], axis=0)
        v = jnp.concatenate([r[:, v_at] for r in pairs + strided], axis=0)
        scores = lax.dot_general(k, q, NT, preferred_element_type=jnp.float32)
        wide = GROUP * BLK
        key_row = lax.broadcasted_iota(jnp.int32, (BLK, wide), 0)
        query_row = lax.broadcasted_iota(jnp.int32, (BLK, wide), 1) % BLK
        rows = []
        for slot in range(12):
            cells = []
            for half in range(2):
                query_block = blocks[half]
                if slot < 8:
                    key_block = blocks[slot % 2] - 2 * (slot // 2)
                    gap = query_block - key_block
                    ok = (key_block >= 0) & (gap >= 0) & (gap < WIN)
                    ok = ok & ((gap < window) | (key_block % stride == 0))
                else:
                    key_block = STRIDE * (group - (slot - 8))
                    ok = (key_block >= 0) & (key_block <= query_block - WIN)
                    ok = ok & (key_block % stride == 0)
                cell = scores[slot * BLK : (slot + 1) * BLK, half * wide : (half + 1) * wide]
                if slot == half:
                    cell = jnp.where(key_row <= query_row, cell, NEG)
                else:
                    cell = jnp.where(ok, cell, NEG)
                cells.append(cell)
            rows.append(jnp.concatenate(cells, axis=1))
        scores = jnp.concatenate(rows, axis=0)
        peak = jnp.max(scores, axis=0, keepdims=True)
        weights = jnp.exp2((scores - peak) * (SCALE * LOG2E))
        probs = weights * (1.0 / jnp.sum(weights, axis=0, keepdims=True))
        grad_prob = lax.dot_general(v, g, NT, preferred_element_type=jnp.float32)
        delta = jnp.sum(probs * grad_prob, axis=0, keepdims=True)
        dscore = (probs * (grad_prob - delta)).astype(jnp.bfloat16)
        dquery = lax.dot_general(dscore, k, TN, preferred_element_type=jnp.float32) * SCALE
        dkey = jnp.dot(dscore, q, preferred_element_type=jnp.float32) * SCALE
        dvalue = jnp.dot(probs.astype(jnp.bfloat16), g, preferred_element_type=jnp.float32)
        for half in range(2):
            for j in range(GROUP):
                at = slice((h * GROUP + j) * HEAD_DIM, (h * GROUP + j + 1) * HEAD_DIM)
                row = (half * GROUP + j) * BLK
                grad = g[row : row + BLK].astype(jnp.float32)
                total = grad + gain[:, at] * dquery[row : row + BLK]
                total = total.astype(jnp.bfloat16)
                both[half, :, at] = total
                if half == 1:
                    other[:, at] = total
        for d in range(4):
            rows_at = slice(2 * BLK * d, 2 * BLK * (d + 1))
            backs[d][:, k_at] = dkey[rows_at].astype(backs[d].dtype)
            backs[d][:, v_at] = dvalue[rows_at].astype(backs[d].dtype)
        for s in range(4):
            rows_at = slice(8 * BLK + BLK * s, 8 * BLK + BLK * (s + 1))
            parts[s][:, k_at] = dkey[rows_at].astype(parts[s].dtype)
            parts[s][:, v_at] = dvalue[rows_at].astype(parts[s].dtype)


WHOLE = pl.BlockSpec(memory_space=pltpu.VMEM)
SCALAR = pl.BlockSpec(memory_space=pltpu.SMEM)
WIDE = 2 * HALF_KV


def shape(dims, dtype):
    return jax.ShapeDtypeStruct(dims, dtype)


def attention(tick, meta, gain, keep, recv, grads, pairs, strided, earlier):
    def at(lead, *rest):
        return pl.BlockSpec((None,) + rest, lambda n: (lead, 0, 0))

    args = [meta, gain, keep, recv]
    specs = [SCALAR, WHOLE, at(tick, BLK, HALF_FEAT), at(tick, BLK, HALF_FEAT)]
    if grads is None:
        args += [keep, recv]
        specs += [at(2, BLK, HALF_FEAT), at(2, BLK, HALF_FEAT)]
    else:
        args += [grads, grads, keep, recv]
        specs += [at(0, BLK, HALF_FEAT), at(1, BLK, HALF_FEAT)]
        specs += [at(3, BLK, HALF_FEAT), at(3, BLK, HALF_FEAT)]
    args += list(pairs) + list(strided)
    specs += [at(tick, 2 * BLK, WIDE)] * 4 + [at(tick, BLK, WIDE)] * 4
    bf16, f32 = jnp.bfloat16, jnp.float32
    out_shape = [shape((2, BLK, HALF_FEAT), bf16)]
    if earlier is None:
        out_shape += [shape((BLK, HALF_FEAT), bf16)] + [shape((2 * BLK, WIDE), bf16)] * 3
    else:
        args += earlier
        specs += [WHOLE] * 4
        out_shape += [shape((2, BLK, HALF_FEAT), bf16)] + [shape((2, 2 * BLK, WIDE), bf16)] * 3
    out_shape += [shape((2 * BLK, WIDE), f32), shape((BLK, WIDE), f32)]
    out_shape += [shape((BLK, WIDE), bf16)] * 3
    return pl.pallas_call(
        functools.partial(attention_kernel, grads is not None),
        out_shape=out_shape,
        grid=(1,),
        in_specs=specs,
        out_specs=[WHOLE] * len(out_shape),
        compiler_params=pltpu.CompilerParams(vmem_limit_bytes=32 << 20),
        cost_estimate=pl.CostEstimate(
            flops=2 * 5 * 2 * 512 * 768 * 128, bytes_accessed=4 << 20, transcendentals=2 * 512 * 768
        ),
        name="attention",
    )(*args)


def simple(kernel, out_shape, args, scalars=1):
    size = sum(a.size * a.dtype.itemsize for a in list(args) + list(out_shape))
    return pl.pallas_call(
        kernel,
        out_shape=out_shape,
        in_specs=[SCALAR] * scalars + [WHOLE] * (len(args) - scalars),
        out_specs=[WHOLE] * len(out_shape),
        compiler_params=pltpu.CompilerParams(vmem_limit_bytes=16 << 20),
        cost_estimate=pl.CostEstimate(flops=size, bytes_accessed=size, transcendentals=0),
        name=kernel.__name__,
    )(*args)


def column_sum(*refs):
    wide_out, send_out = refs[8:]
    for t in range(2):
        total = refs[4 * t][...]
        for s in range(1, 4):
            total = total + refs[4 * t + s][...].astype(jnp.float32)
        wide_out[t] = total
        send_out[t] = total.astype(jnp.bfloat16)


def split_keys(meta, keys, values, keep, give):
    swap = meta[0] % 2 == 1
    for source, at in ((keys, 0), (values, HALF_KV)):
        low, high = source[0, :, :, :HALF_KV], source[0, :, :, HALF_KV:]
        keep[:, :, at : at + HALF_KV] = jnp.where(swap, high, low)
        give[:, :, at : at + HALF_KV] = jnp.where(swap, low, high)


def split_rows(meta, inputs, first, head, keep, give):
    swap = meta[0] % 2 == 1
    for n, source in enumerate((inputs.at[0, 0], inputs.at[0, 1], first.at[0], head.at[0])):
        low, high = source[:, :HALF_FEAT], source[:, HALF_FEAT:]
        keep[n] = jnp.where(swap, high, low)
        give[n] = jnp.where(swap, low, high)


def pair_keys(meta, keep, recv, up_low, up_high, pair, start):
    core = meta[0] % 2
    even = (meta[0] // 8) % 2 == 0
    pair[:, :BLK] = keep[...]
    pair[:, BLK:] = recv[...]
    near = jnp.where(core == 0, keep[...], recv[...])
    above = jnp.where(core == 0, up_low[...], up_high[...])
    start[...] = jnp.where(even, near, above)


def row_sum(meta, *refs):
    total, x1, x2, x3, own0, own1, back1, back2, back3, far_rows = refs[:10]
    mine_out, swap_out, strided_out = refs[10:]
    index = meta[0]
    owner = (index // 2) % 4 == 0
    even = (index // 8) % 2 == 0
    first = (owner & even & (index % 2 == 0)).astype(jnp.float32)
    second = (owner & even & (index % 2 == 1)).astype(jnp.float32)
    for t, own in enumerate((own0, own1)):
        strided = total[t]
        for x in (x1, x2, x3):
            strided = strided + x[t].astype(jnp.float32)
        strided_out[t] = strided.astype(jnp.bfloat16)
        near = own[...]
        for back in (back1, back2, back3):
            near = near + back[t].astype(jnp.float32)
        mine_out[t] = near[:BLK] + first * strided
        swap_out[t, :, :HALF_FEAT] = far_rows[t]
        swap_out[t, :, HALF_FEAT:] = (near[BLK:] + second * strided).astype(jnp.bfloat16)


def finish(meta, mine, swapped, low, high, mine0, mine1, rows_out, keys_out, values_out):
    swap = meta[0] % 2 == 1
    for t, rows in enumerate((mine0, mine1)):
        other = swapped[t, :, HALF_FEAT:].astype(jnp.float32)
        own = (mine[t] + low[t].astype(jnp.float32)).astype(jnp.bfloat16)
        far = (other + high[t].astype(jnp.float32)).astype(jnp.bfloat16)
        left, right = jnp.where(swap, far, own), jnp.where(swap, own, far)
        for out, at in ((keys_out, 0), (values_out, HALF_KV)):
            out[0, t, :, :HALF_KV] = left[:, at : at + HALF_KV]
            out[0, t, :, HALF_KV:] = right[:, at : at + HALF_KV]
        near, far = rows[0], swapped[t, :, :HALF_FEAT]
        rows_out[0, t, :, :HALF_FEAT] = jnp.where(swap, far, near)
        rows_out[0, t, :, HALF_FEAT:] = jnp.where(swap, near, far)


def body(inputs, saved_keys, saved_values, query_gain, first_grads, head_grads, window, stride):
    index = lax.axis_index("ctx")
    section = lax.axis_index("pp")
    last = lax.axis_size("pp") - 1
    core = index % 2
    place = (index // 2) % 4
    f32, bf16 = jnp.float32, jnp.bfloat16

    def ctx(array, move, when=lambda i: True):
        return route(array, "ctx", lambda i: move(i) if when(i) else None)

    spot = index.astype(jnp.int32).reshape(1)
    half = shape((2, BLK, WIDE), bf16)
    kv_keep, kv_give = simple(split_keys, [half, half], [spot, saved_keys, saved_values])
    kv_recv = sibling(kv_give)
    up_low = ctx(kv_keep, lambda i: i + 8, lambda i: i % STRIDE == 0)
    up_high = ctx(kv_give, lambda i: i + 9, lambda i: i % STRIDE == 0)
    pair, start = simple(
        pair_keys,
        [shape((2, 2 * BLK, WIDE), bf16), half],
        [spot, kv_keep, kv_recv, up_low, up_high],
    )
    chosen = start
    for d in range(1, 4):
        across = ctx(start, lambda i: i + 2 * d, lambda i: (i // 2) % 4 == 0)
        chosen = jnp.where(place == d, across, chosen)
    pairs = [pair] + [ctx(pair, lambda i: i + 2 * d) for d in range(1, 4)]

    four = shape((4, BLK, HALF_FEAT), bf16)
    keep, give = simple(split_rows, [four, four], [spot, inputs, first_grads, head_grads])
    recv = sibling(give)
    chosen, recv = lax.optimization_barrier((chosen, recv))
    strided = [chosen] + [ctx(chosen, lambda i: i + STRIDE * s) for s in range(1, 4)]
    gain = jnp.where(core == 0, query_gain[:, :HALF_FEAT], query_gain[:, HALF_FEAT:])
    heads = jnp.where(core == 0, window[0, :2], window[0, 2:])
    steps = jnp.where(core == 0, stride[0, :2], stride[0, 2:])
    top = jnp.where(section == last, 1, 0)
    meta = jnp.concatenate([jnp.stack([index, top]).astype(jnp.int32), heads, steps])

    first = attention(0, meta, gain, keep, recv, None, pairs, strided, None)
    grads = route(first[0], "pp", lambda i: i - 1)
    second = attention(1, meta, gain, keep, recv, grads, pairs, strided, first[1:5])
    columns = []
    for outs in (first, second):
        columns.append(outs[6])
        columns += [ctx(outs[6 + s], lambda i: i - STRIDE * s) for s in range(1, 4)]
    backs = [ctx(second[1 + d], lambda i: i - 2 * d) for d in range(1, 4)]

    wide = shape((2, BLK, WIDE), f32)
    total, send = simple(column_sum, [wide, half], columns, 0)
    rows = [ctx(send, lambda i: i - 2 * d, lambda i: (i // 2) % 4 == d) for d in range(1, 4)]
    mine, swap, down = simple(
        row_sum,
        [wide, shape((2, BLK, HALF_FEAT + WIDE), bf16), half],
        [spot, total] + rows + [first[5], second[5]] + backs + [second[1]],
    )
    swapped = sibling(swap)
    low = ctx(down, lambda i: i - 8, lambda i: i % STRIDE == 8)
    high = ctx(down, lambda i: i - 9, lambda i: i % STRIDE == 9)
    keys_shape = shape(saved_keys.shape, bf16)
    grads_out, key_grads, value_grads = simple(
        finish,
        [shape(inputs.shape, bf16), keys_shape, keys_shape],
        [spot, mine, swapped, low, high, first[0], second[0]],
    )
    return grads_out, key_grads, value_grads


def solution(mesh):
    in_specs = (
        P("pp", None, "ctx", None),
        P("pp", None, "ctx", None),
        P("pp", None, "ctx", None),
        P("pp", None),
        P("pp", "ctx", None),
        P(None, "ctx", None),
        P("pp", None),
        P("pp", None),
    )
    out_specs = (P("pp", None, "ctx", None), P("pp", None, "ctx", None), P("pp", None, "ctx", None))
    return jax.shard_map(body, mesh=mesh, in_specs=in_specs, out_specs=out_specs, check_vma=False)
```
